128 devices in a mesh: seq: 16 (over x, z), seqgrp: 4 (over y_hi, core), fsdp: 2 (over y_lo).
Axes of the slice: x: 4, y: 4 (y_hi: 2, y_lo: 2; y = y_hi * 2 + y_lo), z: 4, core: 2. Of those that a mesh axis runs over, the one named last changes fastest.
Arguments:
- tokens: bfloat16 [8, 2048, 1024], P(('seqgrp', 'fsdp'), 'seq'), may hold values from -6 to 6
- block_order: int32 [32], replicated, may hold values from 0 to 31, as said below
- routes: int32 [8, 2048, 2], P(('seqgrp', 'fsdp'), 'seq'), may hold values from 0 to 2, all different within a row; in each aligned block of 128 rows (0 to 127, 128 to 255, ..., all dimensions but the last counted through in order) at most 96 rows name the same one
- norm1: bfloat16 [1024], P(('seqgrp', 'fsdp')), may hold values from 0.5 to 1.5
- norm2: bfloat16 [1024], P(('seqgrp', 'fsdp')), may hold values from 0.5 to 1.5
- wq: bfloat16 [1024, 1024], P(('seqgrp', 'fsdp')), may hold values from -0.1875 to 0.1875
- wk: bfloat16 [1024, 512], P(('seqgrp', 'fsdp')), may hold values from -0.1875 to 0.1875
- wv: bfloat16 [1024, 512], P(('seqgrp', 'fsdp')), may hold values from -0.1875 to 0.1875
- wo: bfloat16 [1024, 1024], P(('seqgrp', 'fsdp')), may hold values from -1.5 to 1.5
- router: bfloat16 [1024, 3], P(('seqgrp', 'fsdp')), may hold values from -0.09375 to 0.09375
- w_in: bfloat16 [3, 1024, 1024], P(None, ('seqgrp', 'fsdp')), may hold values from -0.1875 to 0.1875
- w_out: bfloat16 [3, 512, 1024], P(None, None, ('seqgrp', 'fsdp')), may hold values from -0.375 to 0.375
- cotangent: bfloat16 [8, 2048, 1024], P(('seqgrp', 'fsdp'), 'seq'), may hold values from -6 to 6
Outputs:
- out: bfloat16 [8, 2048, 1024], P(('seqgrp', 'fsdp'), 'seq')
- grad_tokens: float32 [8, 2048, 1024], P(('seqgrp', 'fsdp'), 'seq')
- grad_norm1: float32 [1024], P(('seqgrp', 'fsdp'))
- grad_norm2: float32 [1024], P(('seqgrp', 'fsdp'))
- grad_wq: float32 [1024, 1024], P(('seqgrp', 'fsdp'))
- grad_wk: float32 [1024, 512], P(('seqgrp', 'fsdp'))
- grad_wv: float32 [1024, 512], P(('seqgrp', 'fsdp'))
- grad_wo: float32 [1024, 1024], P(('seqgrp', 'fsdp'))
- grad_router: float32 [1024, 3], P(('seqgrp', 'fsdp'))
- grad_w_in: float32 [3, 1024, 1024], P(None, ('seqgrp', 'fsdp'))
- grad_w_out: float32 [3, 512, 1024], P(None, None, ('seqgrp', 'fsdp'))
The draws below stay inside these ranges and needn't reach their ends.
Inputs may be any that keep to these rules, and one draw needn't show every extreme that they name: A permutation: slot s of every sequence holds block block_order[s] of 64 tokens, and the two slots 2 i and 2 i + 1 hold blocks that add up to 32 - 1 (one from the front half, its mirror from the back half). `routes`: each token names 2 different experts; among the 128 tokens of one device (aligned blocks of the rows) no expert is named more than 96 times, and exactly 96 times on some device.
All inputs are finite; a program needn't handle non-finite values.
Results may differ from the reference program's by a relative error of at most 0.028.
Values may be sent and summed in bfloat16 or wider, within the bound.
No kernel may reach another device: no remote copies, remote signals or barrier semaphores. Data moves between devices by JAX's collectives and lax.ppermute only.
A program may use at most 128 MiB of HBM per device.

```python
import math
import jax
import jax.numpy as jnp
import numpy as np
from jax import lax

D = 1024
HEADS = 16
KV_HEADS = 8
HD = 64
FF = 512
TOPK = 2
EXPERTS = 3
LENGTH = 2048
SEQS = 8
SLOTS = 32
BLOCK = 64
ROWS_DEV = 128
CAP = 96


def draw_block_order(key, part):
    key = jax.random.fold_in(key, 7)
    pairs = SLOTS // 2
    order_key, flip_key = jax.random.split(key)
    front = jax.random.permutation(order_key, pairs).astype(jnp.int32)
    flips = jax.random.randint(flip_key, (pairs,), 0, 2).astype(jnp.int32)
    mirror = (SLOTS - 1 - front).astype(jnp.int32)
    first = jnp.where(flips == 1, mirror, front)
    second = jnp.where(flips == 1, front, mirror)
    return jnp.stack([first, second], 1).reshape(SLOTS).astype(jnp.int32)


def level_of(key, shape, cuts, least, largest):
    loudness = 1.0
    for axis_at, parts in cuts:
        draws = jax.random.uniform(jax.random.fold_in(jax.random.fold_in(key, 6), axis_at), (parts,), jnp.float32, least / len(cuts), largest / len(cuts))
        loudness = loudness * jnp.repeat(jnp.exp(draws), shape[axis_at] // parts).reshape((-1,) + (1,) * (len(shape) - 1 - axis_at))
    return loudness


def deal_out(own_key, own, number, rows, amount, top, most, skew):
    ranking = jax.random.permutation(own_key, amount)
    heavy_load, ordinary = load_shares(amount, rows * top, most, skew, True), load_shares(amount, rows * top, most, skew, False)
    places = jnp.arange(amount)

    def named(tallies, rotation):
        used = int((tallies > 0).sum())
        fixed = max(1, used // 4)
        shifted = fixed + (places - fixed + rotation * (used - fixed)) % max(1, amount - fixed)
        return jnp.zeros((amount,), jnp.int32).at[ranking[jnp.where(places < fixed, places, shifted)]].set(jnp.asarray(tallies, jnp.int32))

    tallies = jnp.where(number % 4 == 0, named(heavy_load, number // 4), named(ordinary, number - number // 4 - 1))
    mixed = jax.random.permutation(jax.random.fold_in(own, 3), amount)
    donor, taker = mixed[0:amount // 2 * 2:2], mixed[1:amount // 2 * 2:2]
    slack = jnp.minimum(tallies[donor] - 1, most - tallies[taker]) // 2
    slack = jnp.where((donor == ranking[0]) | (taker == ranking[0]) | (tallies[taker] == 0), 0, jnp.maximum(slack, 0))
    shifted = jax.random.randint(jax.random.fold_in(own, 4), (amount // 2,), 0, 1 << 20) % (slack + 1)
    tallies = tallies.at[donor].add(-shifted).at[taker].add(shifted)
    labels = jnp.searchsorted(jnp.cumsum(tallies), jnp.arange(rows * top), side="right").astype(jnp.int32)
    listing = labels.reshape(top, rows).T
    listing = listing[jax.random.permutation(jax.random.fold_in(own, 1), rows)]
    rotation = jax.random.randint(jax.random.fold_in(own, 2), (rows, 1), 0, top)
    return jnp.take_along_axis(listing, (jnp.arange(top)[None, :] + rotation) % top, axis=1)


def load_shares(number_of, total, limit, lean, full):
    weights = [(1 << 20) // math.isqrt(standing ** lean) + 1 for standing in range(1, number_of + 1)]
    largest = limit if full else min(limit, max(-(-total // number_of), total * weights[0] // sum(weights)))
    least = 1 if total - largest >= number_of - 1 else 0
    given, rest = [largest] + [least] * (number_of - 1), total - largest - least * (number_of - 1)
    while rest > 0:
        movable = [i for i in range(1, number_of) if given[i] < largest] or [i for i in range(1, number_of) if given[i] < limit]
        whole, remaining = sum([weights[i] for i in movable]), rest
        for i in movable:
            extra = min(limit - given[i], max(1, remaining * weights[i] // whole), rest)
            given[i] = given[i] + extra
            rest = rest - extra
    return np.array(given)


def noise(own_key, extent, deviation, most, shards=(), kind=jnp.bfloat16):
    array = jax.random.normal(own_key, extent, jnp.float32) * deviation
    if len(shards) > 0:
        array = level_of(own_key, extent, shards, -0.22, 0.18) * array
    return jnp.clip(array, min=-most, max=most).astype(kind)


def setup_inputs(seed: int = 0) -> dict:
    arg_keys = jax.random.split(jax.random.key(seed), 14)
    tokens = noise(arg_keys[0], (SEQS, LENGTH, D), 1.0, 6.0, ((0, 8), (1, 16)))
    block_order = draw_block_order(jax.random.fold_in(arg_keys[13], 71), 0)
    routes_keys = jax.random.split(jax.random.fold_in(arg_keys[2], 1), SEQS * LENGTH // ROWS_DEV)
    routes_turns = jax.random.permutation(jax.random.fold_in(arg_keys[2], 3), SEQS * LENGTH // ROWS_DEV)
    routes = jax.vmap(lambda own, number: deal_out(jax.random.fold_in(arg_keys[2], 2), own, number, ROWS_DEV, EXPERTS, TOPK, CAP, 1))(routes_keys, routes_turns).reshape((SEQS, LENGTH, TOPK))
    norm1 = jnp.clip(1.0 + 0.1 * jax.random.normal(arg_keys[3], (D,), jnp.float32), 0.5, 1.5).astype(jnp.bfloat16)
    norm2 = jnp.clip(1.0 + 0.1 * jax.random.normal(arg_keys[4], (D,), jnp.float32), 0.5, 1.5).astype(jnp.bfloat16)
    wq = noise(arg_keys[5], (D, HEADS * HD), D ** -0.5, 0.1875, ((0, 8),))
    wk = noise(arg_keys[6], (D, KV_HEADS * HD), D ** -0.5, 0.1875, ((0, 8),))
    wv = noise(arg_keys[7], (D, KV_HEADS * HD), D ** -0.5, 0.1875, ((0, 8),))
    wo = noise(arg_keys[8], (HEADS * HD, D), (HEADS * HD // 64) ** -0.5, 1.5, ((0, 8),))
    router = noise(arg_keys[9], (D, EXPERTS), (4 * D) ** -0.5, 0.09375, ((0, 8),))
    w_in = noise(arg_keys[10], (EXPERTS, D, 2 * FF), D ** -0.5, 0.1875, ((1, 8),))
    w_out = noise(arg_keys[11], (EXPERTS, FF, D), (FF // 2) ** -0.5, 0.375, ((2, 8),))
    cotangent = noise(arg_keys[12], (SEQS, LENGTH, D), 1.0, 6.0, ((0, 8), (1, 16)))
    return dict(tokens=tokens, block_order=block_order, routes=routes, norm1=norm1, norm2=norm2, wq=wq, wk=wk, wv=wv, wo=wo, router=router, w_in=w_in, w_out=w_out, cotangent=cotangent)


EPS = 1e-06
THETA = 10000.0
NEG = -1e+30
HIGH = lax.Precision.HIGHEST

@jax.custom_vjp
def low(v):
    return lax.optimization_barrier(v.astype(jnp.bfloat16)).astype(jnp.float32)

@jax.custom_vjp
def low_back(v):
    return v

def low_keep(v):
    return (low(v), None)

def low_pass(kept, grad):
    return (grad,)

def back_keep(v):
    return (v, None)

def back_low(kept, grad):
    return (low(grad),)
low.defvjp(low_keep, low_pass)
low_back.defvjp(back_keep, back_low)

def rotate(values, cosine, sine):
    half = values.shape[-1] // 2
    first = values[..., :half]
    second = values[..., half:]
    return jnp.concatenate([first * cosine - second * sine, second * cosine + first * sine], -1)

def rms(values, gain):
    return values * lax.rsqrt(lax.optimization_barrier(jnp.mean(values * values, -1, keepdims=True)) + EPS) * gain

def forward_seq(params, inputs, route_seq, positions):
    norm1, norm2, wq, wk, wv, wo, router, w_in, w_out = params
    count = inputs.shape[0]
    reps = HEADS // KV_HEADS
    scale = HD ** (-0.5)
    freqs = THETA ** (-(jnp.arange(HD // 2, dtype=jnp.float32) * 2.0) / HD)
    angle = positions.astype(jnp.float32)[:, None] * freqs[None, :]
    cosine = jnp.cos(angle)[:, None, :]
    sine = jnp.sin(angle)[:, None, :]
    normed1 = low(rms(inputs, norm1))
    query = low_back(jnp.dot(normed1, wq, precision=HIGH)).reshape(count, HEADS, HD)
    keys = low_back(jnp.dot(normed1, wk, precision=HIGH)).reshape(count, KV_HEADS, HD)
    values = low(low_back(jnp.dot(normed1, wv, precision=HIGH))).reshape(count, KV_HEADS, HD)
    query = low(rotate(query, cosine, sine)).reshape(count, KV_HEADS, reps, HD)
    keys = low(rotate(keys, cosine, sine))
    width = min(512, count)
    blocks = count // width

    def attend(operands):
        block_query, block_pos = operands
        scores = jnp.einsum('qgrd,kgd->grqk', block_query, keys, precision=HIGH) * scale
        scores = low_back(scores)
        allowed = positions[None, None, None, :] <= block_pos[None, None, :, None]
        scores = jnp.where(allowed, scores, NEG)
        top = lax.optimization_barrier(jnp.max(scores, -1, keepdims=True))
        weights = jnp.exp(scores - top)
        probs = low(weights / lax.optimization_barrier(jnp.sum(weights, -1, keepdims=True)))
        return jnp.einsum('grqk,kgd->qgrd', probs, values, precision=HIGH)
    mixed = lax.map(jax.checkpoint(attend), (query.reshape(blocks, width, KV_HEADS, reps, HD), positions.reshape(blocks, width)))
    mixed = low(low_back(mixed.reshape(count, HEADS * HD)))
    branch = low_back(jnp.dot(mixed, wo, precision=HIGH))
    hidden1 = inputs + branch
    normed2 = low(rms(hidden1, norm2))
    logits = low_back(jnp.dot(normed2, router, precision=HIGH))
    chosen = jnp.take_along_axis(logits, route_seq, 1)
    top = lax.optimization_barrier(jnp.max(chosen, 1, keepdims=True))
    weights = jnp.exp(chosen - top)
    gates = weights / lax.optimization_barrier(jnp.sum(weights, 1, keepdims=True))
    member = (route_seq[:, :, None] == jnp.arange(EXPERTS, dtype=jnp.int32)[None, None, :]).astype(jnp.float32)
    table = lax.optimization_barrier(jnp.sum(member * gates[:, :, None], 1))

    def expert(total, operands):
        win_e, wout_e, column = operands
        joint = low_back(jnp.dot(normed2, win_e, precision=HIGH))
        hidden = low(jax.nn.silu(joint[:, :FF]) * joint[:, FF:])
        result = low_back(jnp.dot(hidden, wout_e, precision=HIGH))
        return (total + column[:, None] * result, None)
    mixture, unused = lax.scan(jax.checkpoint(expert), jnp.zeros_like(inputs), (w_in, w_out, table.T))
    return hidden1 + mixture

def add_pair(first, second):
    return first + second

def reference(tokens, block_order, routes, norm1, norm2, wq, wk, wv, wo, router, w_in, w_out, cotangent):
    positions = (block_order[:, None] * BLOCK + jnp.arange(BLOCK, dtype=jnp.int32)[None, :]).reshape(-1)
    params = (norm1.astype(jnp.float32), norm2.astype(jnp.float32), wq.astype(jnp.float32), wk.astype(jnp.float32), wv.astype(jnp.float32), wo.astype(jnp.float32), router.astype(jnp.float32), w_in.astype(jnp.float32), w_out.astype(jnp.float32))

    def one_sequence(totals, operands):
        seq_tokens, seq_routes, seq_cot = operands

        def forward_here(weights, inputs):
            return forward_seq(weights, inputs, seq_routes, positions)
        result, pullback = jax.vjp(forward_here, params, seq_tokens.astype(jnp.float32))
        grads, grad_inputs = pullback(seq_cot.astype(jnp.float32))
        return (jax.tree.map(add_pair, totals, grads), (result.astype(jnp.bfloat16), grad_inputs))
    zeros = jax.tree.map(jnp.zeros_like, params)
    totals, (outs, grad_inputs) = lax.scan(one_sequence, zeros, (tokens, routes, cotangent))
    return (outs, grad_inputs, totals[0], totals[1], totals[2], totals[3], totals[4], totals[5], totals[6], totals[7], totals[8])
```

```python
import functools

import jax
import jax.numpy as jnp
from jax import lax
from jax.experimental import pallas as pl
from jax.experimental.pallas import tpu as pltpu
from jax.sharding import PartitionSpec as P

HEADS = 16
KV_HEADS = 8
HD = 64
FF = 512
EXPERTS = 3
EPS = 1e-06
THETA = 10000.0
NEG = -1e30
Y = ("seqgrp", "fsdp")
CORE = 2
HOPS = (1, 5, 4)
OWN = (0, 1, 5, 4)
BF = jnp.bfloat16
F32 = jnp.float32
VMEM = 56 * 1024 * 1024


def dot(left, right):
    return jnp.dot(left, right, preferred_element_type=F32)


def dot_cols(left, right):
    return lax.dot_general(left, right, (((1,), (1,)), ((), ())), preferred_element_type=F32)


def dot_rows(left, right):
    return lax.dot_general(left, right, (((0,), (0,)), ((), ())), preferred_element_type=F32)


def lanes(rows, width=128):
    return lax.broadcasted_iota(jnp.int32, (rows, width), 1)


def swap_halves(u):
    lane = lanes(u.shape[0])
    return jnp.where((lane & 63) < 32, pltpu.roll(u, 96, 1), pltpu.roll(u, 32, 1))


def call(kernel, out_shape, scratch=(), smem=0, cost=None):
    def run(*args):
        count = len(args)
        return pl.pallas_call(
            kernel,
            out_shape=out_shape,
            in_specs=[pl.BlockSpec(memory_space=pltpu.SMEM)] * smem
            + [pl.BlockSpec(memory_space=pltpu.VMEM)] * (count - smem),
            out_specs=jax.tree.map(lambda _: pl.BlockSpec(memory_space=pltpu.VMEM), out_shape),
            scratch_shapes=list(scratch),
            compiler_params=pltpu.CompilerParams(vmem_limit_bytes=VMEM),
            cost_estimate=cost,
        )(*args)

    return run


def shape(*dims, kind=BF):
    return jax.ShapeDtypeStruct(dims, kind)


def cost(us):
    return pl.CostEstimate(flops=0, bytes_accessed=int(us * 3_600_000), transcendentals=0)


def pairs(k):
    return [(i, i ^ k) for i in range(8)]


def hop(x, k):
    return lax.ppermute(x, Y, pairs(k))


def gather_far(x):
    return {k: hop(x, k) for k in (4, 5, 1)}


def gather_near(x, far, *ready):
    parts = {0: x, CORE: hop(x, CORE), **far}
    for k in HOPS:
        parts[k ^ CORE] = hop(after(far[k], *ready) if k == 1 else far[k], CORE)
    return [parts[k] for k in range(8)]


def gather_group(x, *ready):
    return gather_near(x, gather_far(x), *ready)


def scatter_start(*blocks):
    mine, other = blocks[:4], hop(blocks[4], CORE)
    sums = [mine[i].astype(F32) + other[i].astype(F32) for i in range(4)]
    return [sums[0]] + [sums[i].astype(BF) for i in (1, 2, 3)]


def scatter_end(sums):
    return [sums[0]] + [hop(sums[i], OWN[i]) for i in (3, 2, 1)]


def total(parts):
    return parts[0] + sum(p.astype(F32) for p in parts[1:])


def after(x, *earlier):
    return lax.optimization_barrier((x,) + earlier)[0]


def norm_rows(x):
    return lax.rsqrt(jnp.mean(x * x, 1, keepdims=True) + EPS)


def join(even, odd):
    first = lanes(even.shape[0]) < 64
    even, odd = even.astype(F32), odd.astype(F32)
    low = jnp.where(first, even, pltpu.roll(odd, 64, 1))
    high = jnp.where(first, pltpu.roll(even, 64, 1), odd)
    return low.astype(BF), high.astype(BF)


def prepare_kernel(at_ref, wq_ref, wk_ref, wv_ref, small_ref, in_ref, out_ref, pay_ref):
    for t in range(4):
        at = slice(128 * t, 128 * t + 128)
        up = slice(512 + 128 * t, 640 + 128 * t)
        pay_ref[2 * t, 128:256, :], pay_ref[2 * t + 1, 128:256, :] = join(wk_ref[:, at], wv_ref[:, at])
        pay_ref[2 * t, 272:304, :], pay_ref[2 * t + 1, 272:304, :] = join(in_ref[0, :, at], in_ref[0, :, up])
    for y in range(8):
        pay_ref[y, :128, :] = wq_ref[:, 128 * y : 128 * y + 128]
        pay_ref[y, 256:272, :] = small_ref[...]
        pay_ref[y, 304:320, :] = out_ref[0, y]


def prepare(seq, wq, wk, wv, small, w_in, w_out):
    piece = jnp.minimum(seq, 11)
    at = jnp.stack([piece // 4, piece % 4]).astype(jnp.int32)

    def whole(*dims):
        return pl.BlockSpec(dims, lambda i, ref: (0,) * len(dims))

    return pl.pallas_call(
        prepare_kernel,
        grid_spec=pltpu.PrefetchScalarGridSpec(
            num_scalar_prefetch=1,
            grid=(1,),
            in_specs=[
                whole(128, 1024),
                whole(128, 512),
                whole(128, 512),
                whole(16, 128),
                pl.BlockSpec((1, 32, 1024), lambda i, ref: (ref[0], ref[1], 0)),
                pl.BlockSpec((1, 8, 16, 128), lambda i, ref: (ref[0], 0, ref[1], 0)),
            ],
            out_specs=whole(8, 320, 128),
        ),
        out_shape=shape(8, 320, 128),
        compiler_params=pltpu.CompilerParams(vmem_limit_bytes=VMEM),
        cost_estimate=cost(20),
    )(at, wq, wk, wv, small, w_in, w_out.reshape(3, 8, 64, 128))


def arrange_weights_kernel(all_ref, w1_ref, w2_ref):
    w2_ref[192:256, :] = jnp.zeros((64, 1024), BF)
    for y in range(8):
        ends = []
        for e in range(EXPERTS):
            ends.append(
                jnp.concatenate([all_ref[4 * e + i, y, :32, :] for i in range(4)], 0)
            )
        span = slice(128 * y, 128 * y + 128)
        low, high = join(ends[0], ends[1])
        w1_ref[span, :128] = low
        w1_ref[span, 256:384] = high
        low, high = join(ends[2], jnp.zeros_like(ends[2]))
        w1_ref[span, 128:256] = low
        w1_ref[span, 384:512] = high
        for s in range(12):
            w2_ref[16 * s : 16 * s + 16, span] = all_ref[s, y, 32:48, :]


def qkv_kernel(*refs):
    xs, (all_ref, cos_ref, sin_ref, pay_ref, w_ref, n_ref, small_ref) = refs[:8], refs[8:]
    for y in range(8):
        w_ref[128 * y : 128 * y + 128, :128] = all_ref[y, :128, :]
        w_ref[128 * y : 128 * y + 128, 128:] = all_ref[y, 128:256, :]
        small_ref[:, 128 * y : 128 * y + 128] = all_ref[y, 256:272, :].astype(F32)
    gain = small_ref[0:1, :]
    cosine, sine = cos_ref[...], sin_ref[...]
    first = lanes(128) < 64
    for pair in range(4):
        x = jnp.concatenate([xs[2 * pair][...], xs[2 * pair + 1][...]], 0).astype(F32)
        normed = (x * norm_rows(x) * gain).astype(BF)
        n_ref[256 * pair : 256 * pair + 256, :] = normed
        both = dot(normed, w_ref[...])
        for i in range(2):
            k = 2 * pair + i
            query = both[128 * i : 128 * i + 128, :128]
            kv = both[128 * i : 128 * i + 128, 128:]
            query = ((query * cosine + swap_halves(query) * sine) * HD**-0.5).astype(BF)
            kv = jnp.where(first, kv * cosine + swap_halves(kv) * sine, kv).astype(BF)
            for half in range(2):
                for slot in range(2):
                    at = slot * 64 + half * 32
                    pay_ref[2 * k + half, slot * 32 : slot * 32 + 32, :] = query[at : at + 32]
                pay_ref[2 * k + half, 64:192, :] = kv


def double(kv):
    kv = kv.astype(F32)
    rolled = pltpu.roll(kv, 64, 1)
    first = lanes(kv.shape[0]) < 64
    return jnp.where(first, kv, rolled), jnp.where(first, rolled, kv)


def stack_heads(rows):
    first = lanes(rows.shape[0]) < 64
    zero = jnp.zeros_like(rows)
    return jnp.concatenate([jnp.where(first, rows, zero), jnp.where(first, zero, rows)], 0)


def merge_heads(stacked):
    half = stacked.shape[0] // 2
    return jnp.where(lanes(half) < 64, stacked[:half], stacked[half:])


def causal(half):
    key = lax.broadcasted_iota(jnp.int32, (256, 256), 0)
    row = lax.broadcasted_iota(jnp.int32, (256, 256), 1) & 127
    return key <= (row >> 5) * 64 + half * 32 + (row & 31)


def scores_of(k2, stacked, n, mask):
    raw = dot_cols(k2[:n], stacked)
    last = jnp.where(mask, raw[n - 256 :], NEG)
    return last if n == 256 else jnp.concatenate([raw[: n - 256], last], 0)


def place(order_ref, p):
    slot = order_ref[p]
    return slot >> 1, slot & 1


def attend_kernel(order_ref, pay_ref, out_ref, sorted_ref, log_ref, q_ref, kv_ref, k2_ref, v2t_ref):
    for p in range(32):
        s, i = place(order_ref, p)
        q_ref[32 * p : 32 * p + 32, :] = pay_ref[s, pl.ds(pl.multiple_of(i * 32, 32), 32), :]
        kv_ref[64 * p : 64 * p + 64, :] = pay_ref[s, pl.ds(pl.multiple_of(64 + i * 64, 64), 64), :]
    for j in range(8):
        k2, v2 = double(kv_ref[256 * j : 256 * j + 256, :])
        k2_ref[256 * j : 256 * j + 256, :] = k2.astype(BF)
        v2t_ref[:, 256 * j : 256 * j + 256] = v2.T.astype(BF)
    mask = causal(order_ref[32])
    for c in range(8):
        n = 256 * (c + 1)
        stacked = stack_heads(q_ref[128 * c : 128 * c + 128, :])
        scores = scores_of(k2_ref, stacked, n, mask)
        top = jnp.max(scores, 0, keepdims=True)
        weights = jnp.exp(scores - top)
        total = jnp.sum(weights, 0, keepdims=True)
        mixed = dot(v2t_ref[:, :n], weights.astype(BF)) / total
        log_ref[c : c + 1, :] = top + jnp.log(total)
        mixed = merge_heads(mixed.T)
        sorted_ref[128 * c : 128 * c + 128, :] = mixed
        for r in range(4):
            s, i = place(order_ref, 4 * c + r)
            out_ref[s, pl.ds(pl.multiple_of(i * 32, 32), 32), :] = mixed[32 * r : 32 * r + 32].astype(BF)


def attend_back_kernel(
    order_ref, dmix_ref, sorted_ref, log_ref, q_ref, kv_ref, out_ref, k2_ref, k2t_ref, v2_ref, dk_ref, dv_ref, d_ref
):
    for p in range(32):
        s, i = place(order_ref, p)
        d_ref[32 * p : 32 * p + 32, :] = dmix_ref[s, pl.ds(pl.multiple_of(i * 32, 32), 32), :]
    for j in range(8):
        k2, v2 = double(kv_ref[256 * j : 256 * j + 256, :])
        k2_ref[256 * j : 256 * j + 256, :] = k2.astype(BF)
        v2_ref[256 * j : 256 * j + 256, :] = v2.astype(BF)
        k2t_ref[:, 256 * j : 256 * j + 256] = k2.T.astype(BF)
    mask = causal(order_ref[32])
    for c in reversed(range(8)):
        n = 256 * (c + 1)
        stacked = stack_heads(q_ref[128 * c : 128 * c + 128, :])
        dmix = d_ref[128 * c : 128 * c + 128, :]
        dstacked = stack_heads(dmix)
        product = dmix.astype(F32) * sorted_ref[128 * c : 128 * c + 128, :]
        delta = jnp.sum(stack_heads(product).T, 0, keepdims=True)
        scores = scores_of(k2_ref, stacked, n, mask)
        probs = jnp.exp(scores - log_ref[c : c + 1, :])
        dprobs = dot_cols(v2_ref[:n], dstacked)
        dscores = (probs * (dprobs - delta)).astype(BF)
        dkeys = dot(dscores, stacked)
        dvalues = dot(probs.astype(BF), dstacked)
        if c == 7:
            dk_ref[...] = dkeys
            dv_ref[...] = dvalues
        else:
            dk_ref[:n] += dkeys
            dv_ref[:n] += dvalues
        dquery = merge_heads(dot(k2t_ref[:, :n], dscores).T) * HD**-0.5
        for r in range(4):
            s, i = place(order_ref, 4 * c + r)
            out_ref[s, pl.ds(pl.multiple_of(i * 32, 32), 32), :] = dquery[32 * r : 32 * r + 32].astype(BF)
    first = lanes(64) < 64
    for p in range(32):
        s, i = place(order_ref, p)
        dk = dk_ref[64 * p : 64 * p + 64, :]
        dv = dv_ref[64 * p : 64 * p + 64, :]
        both = jnp.where(first, dk + pltpu.roll(dk, 64, 1), dv + pltpu.roll(dv, 64, 1))
        out_ref[s, pl.ds(pl.multiple_of(64 + i * 64, 64), 64), :] = both.astype(BF)


def rows_of(ref, k):
    return jnp.concatenate(
        [ref[2 * k + half, slot * 32 : slot * 32 + 32, :] for slot in range(2) for half in range(2)], 0
    )


def expand(table):
    lane = lanes(table.shape[0], 256)
    return jnp.where(
        lane < 64,
        table[:, 0:1],
        jnp.where(lane < 128, table[:, 1:2], jnp.where(lane < 192, table[:, 2:3], 0.0)),
    )


CHUNK = 2


def split_blocks(block, k, mine_refs, other_ref):
    if k & CORE:
        other_ref[OWN.index(k ^ CORE)] = block
    else:
        mine_refs[OWN.index(k)][...] = block


def split_shapes():
    return (shape(128, 1024),) * 4 + (shape(4, 128, 1024),)


def expert_kernel(*refs):
    xs, mixes, wos, cots = refs[:8], refs[8:16], refs[16:24], refs[24:32]
    w1_ref, w2_ref, small_ref, router_ref = refs[32:36]
    hid_ref, pay_ref = refs[36:38]
    mine_refs, other_ref, mmine_refs, mother_ref = refs[38:42], refs[42], refs[43:47], refs[47]
    wo_ref, n_ref, dj_ref, cot_ref, hg_ref = refs[48:]
    for m in range(8):
        wo_ref[128 * m : 128 * m + 128, :] = wos[m][...]
        cot_ref[128 * m : 128 * m + 128, :] = cots[m][:, :1024]
    rows = 128 * CHUNK
    gain = small_ref[1:2, :]
    gain_grad = jnp.zeros((1, 1024), F32)
    lane = lanes(rows)
    lane2 = lanes(rows, 256)
    for first in range(0, 8, CHUNK):
        ks = range(first, first + CHUNK)
        span = slice(128 * first, 128 * first + rows)
        x = jnp.concatenate([xs[k][...] for k in ks], 0).astype(F32)
        mixed = jnp.concatenate(
            [
                jnp.concatenate([rows_of(mixes[m], k ^ m) for m in range(8)], 1)
                for k in ks
            ],
            0,
        )
        hidden1 = x + dot(mixed, wo_ref[...])
        if first == 0:
            hid_ref[...] = hidden1[:128]
        unit = hidden1 * norm_rows(hidden1)
        normed = (unit * gain).astype(BF)
        n_ref[span, :] = normed
        joint = dot(normed, w1_ref[...])
        logits = dot_cols(normed, router_ref[...])
        member = jnp.concatenate([cots[k][:, 1024:] for k in ks], 0).astype(F32) > 0.5
        logits = jnp.where(member, logits, NEG)
        weights = jnp.where(member, jnp.exp(logits - jnp.max(logits, 1, keepdims=True)), 0.0)
        gates = weights / jnp.sum(weights, 1, keepdims=True)
        spread = expand(gates)
        gate, up = joint[:, :256], joint[:, 256:]
        sigma = jax.nn.sigmoid(gate)
        active = gate * sigma
        hidden = (active * up).astype(BF).astype(F32)
        gated = (hidden * spread).astype(BF)
        hg_ref[span, :] = gated
        mixture = dot(gated, w2_ref[...]).astype(BF)
        draw = dot_cols(cot_ref[span, :], w2_ref[...])
        product = hidden * draw
        dgates = jnp.zeros((rows, 128), F32)
        for e in range(EXPERTS):
            part = jnp.sum(jnp.where((lane2 >> 6) == e, product, 0.0), 1, keepdims=True)
            dgates = jnp.where(lane == e, part, dgates)
        dlogits = (gates * (dgates - jnp.sum(gates * dgates, 1, keepdims=True))).astype(BF)
        dhidden = draw * spread
        slope = sigma * (1.0 + gate * (1.0 - sigma))
        djoint = jnp.concatenate([dhidden * up * slope, dhidden * active], 1).astype(BF)
        dj_ref[span, :512] = djoint
        dj_ref[span, 512:] = dlogits
        dnormed = dot_cols(djoint, w1_ref[...]) + dot(dlogits, router_ref[...])
        gain_grad += jnp.sum(dnormed * unit, 0, keepdims=True)
        dnormed = dnormed.astype(BF)
        for i, k in enumerate(ks):
            split_blocks(dnormed[128 * i : 128 * i + 128], k, mine_refs, other_ref)
            split_blocks(mixture[128 * i : 128 * i + 128], k, mmine_refs, mother_ref)
    grad1 = dot_rows(dj_ref[...], n_ref[...])
    pay_ref[:192, :] = grad1[:192].astype(BF)
    pay_ref[192:384, :] = grad1[256:448].astype(BF)
    last = grad1[512:576]
    row = lax.broadcasted_iota(jnp.int32, last.shape, 0)
    pay_ref[576:640, :] = jnp.where(row == 3, gain_grad, last).astype(BF)
    pay_ref[384:576, :] = dot_rows(hg_ref[...], cot_ref[...])[:192].astype(BF)


def norm_back(values, gain, dnormed):
    scale = norm_rows(values)
    unit = values * scale
    dunit = dnormed * gain
    return scale * (dunit - unit * jnp.mean(dunit * unit, 1, keepdims=True))


def branch_kernel(me_ref, *refs):
    parts, (hid_ref, cot_ref, small_ref, grad_ref) = refs[:4], refs[4:8]
    wos, (dhid_ref, dbranch_ref, pay_ref) = refs[8:16], refs[16:]
    dnormed = parts[0][...] + sum(p[...].astype(F32) for p in parts[1:])
    dhidden = cot_ref[...].astype(F32) + norm_back(hid_ref[...], small_ref[1:2, :], dnormed)
    dhid_ref[...] = dhidden
    dbranch = dhidden.astype(BF)
    dbranch_ref[...] = dbranch
    for m in range(8):
        pay_ref[me_ref[0] ^ m, :128, :] = dot_cols(dbranch, wos[m][...]).astype(BF)
    grad = jnp.zeros((40, 1024), F32)
    for s in range(16):
        grad += grad_ref[s].astype(F32)
    grad = jnp.concatenate([grad, jnp.zeros((8, 1024), F32)], 0).astype(BF)
    for y in range(8):
        pay_ref[y, 128:, :] = grad[:, 128 * y : 128 * y + 128]


def tokens_kernel(*refs):
    parts, (x_ref, dhid_ref, small_ref, out_ref) = refs[:4], refs[4:]
    dnormed = parts[0][...] + sum(p[...].astype(F32) for p in parts[1:])
    out_ref[...] = dhid_ref[...] + norm_back(x_ref[...].astype(F32), small_ref[0:1, :], dnormed)


def arrange_kernel(me_ref, in_ref, pay_ref):
    for k in range(8):
        block = in_ref[me_ref[0] ^ k, :128, :]
        for half in range(2):
            for slot in range(2):
                at = slot * 64 + half * 32
                pay_ref[2 * k + half, slot * 32 : slot * 32 + 32, :] = block[at : at + 32]


def branch_grad_kernel(*refs):
    ds, (mix_ref, g_ref, all_ref) = refs[:8], refs[8:]
    for k in range(8):
        all_ref[128 * k : 128 * k + 128, :] = ds[k][...]
    mixed = jnp.concatenate([rows_of(mix_ref, k) for k in range(8)], 0)
    g_ref[...] = dot_rows(mixed, all_ref[...]).T.astype(BF)


def qkv_back_kernel(*refs):
    xs, (pay_ref, n_ref, cos_ref, sin_ref, gwo_ref, w_ref) = refs[:8], refs[8:14]
    g_ref, gn_ref, mine_refs, other_ref, d_ref = refs[14], refs[15], refs[16:20], refs[20], refs[21]
    cosine, sine = cos_ref[...], sin_ref[...]
    first = lanes(128) < 64
    for k in range(8):
        at = 128 * k
        dquery = rows_of(pay_ref, k).astype(F32)
        dquery = dquery * cosine - swap_halves(dquery) * sine
        dkv = pay_ref[2 * k, 64:192, :].astype(F32) + pay_ref[2 * k + 1, 64:192, :].astype(F32)
        dkv = jnp.where(first, dkv * cosine - swap_halves(dkv) * sine, dkv)
        d_ref[at : at + 128, :128] = dquery.astype(BF)
        d_ref[at : at + 128, 128:] = dkv.astype(BF)
    grad = dot_rows(d_ref[...], n_ref[...]).astype(BF)
    for s in range(16):
        for y in range(8):
            g_ref[s, 16 * y : 16 * y + 16, :] = grad[16 * s : 16 * s + 16, 128 * y : 128 * y + 128]
        g_ref[s, 128:, :] = gwo_ref[64 * s : 64 * s + 64, :]
    gain_grad = jnp.zeros((1, 1024), F32)
    for pair in range(4):
        x = jnp.concatenate([xs[2 * pair][...], xs[2 * pair + 1][...]], 0).astype(F32)
        dnormed = dot_cols(d_ref[256 * pair : 256 * pair + 256, :], w_ref[...])
        gain_grad += jnp.sum(dnormed * (x * norm_rows(x)), 0, keepdims=True)
        dnormed = dnormed.astype(BF)
        for i in range(2):
            split_blocks(dnormed[128 * i : 128 * i + 128], 2 * pair + i, mine_refs, other_ref)
    for y in range(8):
        part = gain_grad[:, 128 * y : 128 * y + 128]
        gn_ref[y] = jnp.broadcast_to(part, (16, 128)).astype(BF)


def qkv_final_kernel(all_ref, q_ref, k_ref, v_ref, wo_ref, gn_ref):
    first = lanes(128) < 64
    total = jnp.zeros((16, 128), F32)
    for s in range(16):
        total += all_ref[s, 128:144, :].astype(F32)
    gn_ref[...] = total[0:1]
    for s in range(0, 16, 2):
        rows = jnp.concatenate([all_ref[s, 144:208, :], all_ref[s + 1, 144:208, :]], 0)
        wo_ref[:, 64 * s : 64 * s + 128] = rows.astype(F32).T
    for t in range(4):
        tails = []
        for y in (2 * t, 2 * t + 1):
            rows = jnp.concatenate([all_ref[s, 16 * y : 16 * y + 16, :] for s in range(16)], 0)
            turned = rows.astype(F32).T
            q_ref[:, 128 * y : 128 * y + 128] = turned[:, :128]
            tails.append(turned[:, 128:])
        even, odd = tails
        k_ref[:, 128 * t : 128 * t + 128] = jnp.where(first, even, pltpu.roll(odd, 64, 1))
        v_ref[:, 128 * t : 128 * t + 128] = jnp.where(first, pltpu.roll(even, 64, 1), odd)


def expert_final_kernel(all_ref, win_ref, wout_ref, router_ref, gn_ref):
    for e in range(EXPERTS):
        for part in range(2):
            at = part * 192 + e * 64
            for t in range(4):
                rows = jnp.concatenate(
                    [all_ref[2 * t, at : at + 64, :], all_ref[2 * t + 1, at : at + 64, :]], 0
                )
                win_ref[e, :, part * 512 + 128 * t : part * 512 + 128 * t + 128] = rows.astype(F32).T
        for y in range(8):
            at = 384 + e * 64
            wout_ref[e, 64 * y : 64 * y + 64, :] = all_ref[y, at : at + 64, :].astype(F32)
    total = jnp.zeros((16, 128), F32)
    for y in range(8):
        total += all_ref[y, 576:592, :].astype(F32)
    router_ref[...] = total.T[:, :3]
    gn_ref[...] = total[3:4]


def swap_seq(x):
    return lax.all_to_all(x, "seq", 0, 0)


def swap_group(x):
    return lax.all_to_all(x, Y, 0, 0)


def spread_seq(x):
    return swap_seq(jnp.broadcast_to(x[None], (16,) + x.shape))


def local(
    tokens, block_order, routes, norm1, norm2, wq, wk, wv, wo, router, w_in, w_out, cotangent
):
    here = tokens[0]
    seq = lax.axis_index("seq")

    slots = lax.dynamic_slice_in_dim(block_order, 2 * seq, 2)
    position = (slots[:, None] * 64 + jnp.arange(64, dtype=jnp.int32)[None, :]).reshape(-1)
    freqs = THETA ** (-(jnp.arange(HD // 2, dtype=F32) * 2.0) / HD)
    angle = position.astype(F32)[:, None] * jnp.tile(freqs, 4)[None, :]
    cosine = jnp.cos(angle)
    sine = jnp.where((jnp.arange(128) & 63)[None, :] < 32, -jnp.sin(angle), jnp.sin(angle))
    index = jnp.arange(32, dtype=jnp.int32)
    order = jnp.sum(jnp.where(block_order[None, :] == index[:, None], index[None, :], 0), 1)
    order = jnp.concatenate([order, (seq & 1)[None].astype(jnp.int32)])
    member = jnp.any(
        routes[0][:, :, None] == jnp.arange(128, dtype=jnp.int32)[None, None, :], 1
    ).astype(BF)
    cot_member = jnp.concatenate([cotangent[0], member], 1)

    xs = gather_group(here)
    small = jnp.concatenate([norm1[None], norm2[None], router.T, jnp.zeros((11, 128), BF)], 0)
    weights = prepare(seq, wq, wk, wv, small, w_in, w_out)
    weights = swap_group(after(weights, xs[1], xs[5], xs[4], cosine, sine, order, cot_member))

    payload, w_qkv, normed1, gains = call(
        qkv_kernel,
        (shape(16, 192, 128), shape(1024, 256), shape(1024, 1024), shape(16, 1024, kind=F32)),
        cost=cost(1),
    )(*xs, weights, cosine, sine)

    expert_all = lax.all_gather(weights[:, 272:], "seq")
    w1, w2 = call(
        arrange_weights_kernel, (shape(1024, 512), shape(256, 1024)), cost=cost(1)
    )(expert_all)
    router_t = jnp.pad(gains[2:5].astype(BF), ((0, 125), (0, 0)))

    payload = swap_seq(payload)
    mixed_back, mixed_sorted, logs, q_sorted, kv_sorted = call(
        attend_kernel,
        (
            shape(16, 64, 128),
            shape(1024, 128, kind=F32),
            shape(8, 256, kind=F32),
            shape(1024, 128),
            shape(2048, 128),
        ),
        scratch=[pltpu.VMEM((2048, 128), BF), pltpu.VMEM((128, 2048), BF)],
        smem=1,
        cost=cost(1),
    )(order, payload)
    cots = gather_group(after(cot_member, xs[4]))
    wos = gather_group(after(wo, cots[4]))
    mixed_own = swap_seq(mixed_back)
    mixes = gather_group(mixed_own, w1, w2, router_t)
    hidden1, grad_pay, *partial = call(
        expert_kernel,
        (shape(128, 1024, kind=F32), shape(640, 1024)) + split_shapes() + split_shapes(),
        scratch=[
            pltpu.VMEM((1024, 1024), BF),
            pltpu.VMEM((1024, 1024), BF),
            pltpu.VMEM((1024, 640), BF),
            pltpu.VMEM((1024, 1024), BF),
            pltpu.VMEM((1024, 256), BF),
        ],
        cost=cost(1),
    )(*xs, *mixes, *wos, *cots, w1, w2, gains, router_t)

    grad_pay = swap_seq(grad_pay.reshape(16, 40, 1024))
    dn_parts = scatter_end(scatter_start(*partial[:5]))

    me = lax.axis_index(Y).astype(jnp.int32)
    dhidden1, dbranch, dmixed = call(
        branch_kernel,
        (shape(128, 1024, kind=F32), shape(128, 1024), shape(8, 176, 128)),
        smem=1,
        cost=cost(1),
    )(me[None], *dn_parts, hidden1, cotangent[0], gains, grad_pay, *wos)
    dmixed = swap_group(dmixed)
    dmix_pay = call(arrange_kernel, shape(16, 64, 128), smem=1, cost=cost(1))(me[None], dmixed)

    dbranch_far = gather_far(after(dbranch, dmixed))
    dmix_pay = after(swap_seq(dmix_pay), *dbranch_far.values())
    back_pay = call(
        attend_back_kernel,
        shape(16, 192, 128),
        scratch=[
            pltpu.VMEM((2048, 128), BF),
            pltpu.VMEM((128, 2048), BF),
            pltpu.VMEM((2048, 128), BF),
            pltpu.VMEM((2048, 128), F32),
            pltpu.VMEM((2048, 128), F32),
            pltpu.VMEM((1024, 128), BF),
        ],
        smem=1,
        cost=cost(1),
    )(order, dmix_pay, mixed_sorted, logs, q_sorted, kv_sorted)

    expert_grads = lax.all_gather(dmixed[:, 128:168], "seq", axis=1, tiled=True)
    part_win, part_wout, part_router, part_gain2 = call(
        expert_final_kernel,
        (
            shape(3, 128, 1024, kind=F32),
            shape(3, 512, 128, kind=F32),
            shape(128, 3, kind=F32),
            shape(1, 128, kind=F32),
        ),
        cost=cost(1),
    )(expert_grads)

    dbranches = gather_near(after(dbranch, back_pay), dbranch_far, back_pay)
    grad_wo = call(
        branch_grad_kernel,
        shape(1024, 128),
        scratch=[pltpu.VMEM((1024, 1024), BF)],
        cost=cost(1),
    )(*dbranches, mixed_own)
    mix_parts = scatter_end(scatter_start(*partial[5:9], after(partial[9], dmix_pay)))
    back_pay = after(swap_seq(back_pay), *mix_parts)
    outcome = (hidden1 + total(mix_parts)).astype(BF)
    grad_qkv, grad_gain1, *partial = call(
        qkv_back_kernel,
        (shape(16, 192, 128), shape(8, 16, 128)) + split_shapes(),
        scratch=[pltpu.VMEM((1024, 256), BF)],
        cost=cost(2),
    )(*xs, back_pay, normed1, cosine, sine, grad_wo, w_qkv)
    dn_parts = scatter_end(scatter_start(*partial))
    grad_qkv = after(swap_seq(grad_qkv), *dn_parts)
    qkv_sum = jnp.sum(grad_qkv.astype(F32), 0).astype(BF)
    wo_sum = qkv_sum[128:]
    qkv_part = swap_group(jnp.concatenate([qkv_sum[:128].reshape(8, 16, 128), grad_gain1], 1))
    grad_inputs = call(
        tokens_kernel, shape(128, 1024, kind=F32), cost=cost(1)
    )(*dn_parts, here, dhidden1, gains)
    qkv_part = after(qkv_part, grad_inputs, outcome)
    gain1_part = jnp.sum(qkv_part[:, 16:].astype(F32), 0).astype(BF)
    qkv_all = spread_seq(
        jnp.concatenate(
            [qkv_part[:, :16].reshape(128, 128), gain1_part, wo_sum], 0
        )
    )
    part_q, part_k, part_v, part_wo, part_gain1 = call(
        qkv_final_kernel,
        (
            shape(128, 1024, kind=F32),
            shape(128, 512, kind=F32),
            shape(128, 512, kind=F32),
            shape(128, 1024, kind=F32),
            shape(1, 128, kind=F32),
        ),
        cost=cost(1),
    )(after(qkv_all, part_win))

    return (
        outcome[None],
        grad_inputs[None],
        part_gain1[0],
        part_gain2[0],
        part_q,
        part_k,
        part_v,
        part_wo,
        part_router,
        part_win,
        part_wout,
    )


def solution(mesh):
    return jax.shard_map(
        local,
        mesh=mesh,
        in_specs=(
            P(("seqgrp", "fsdp"), "seq", None),
            P(),
            P(("seqgrp", "fsdp"), "seq", None),
            P(("seqgrp", "fsdp")),
            P(("seqgrp", "fsdp")),
            P(("seqgrp", "fsdp"), None),
            P(("seqgrp", "fsdp"), None),
            P(("seqgrp", "fsdp"), None),
            P(("seqgrp", "fsdp"), None),
            P(("seqgrp", "fsdp"), None),
            P(None, ("seqgrp", "fsdp"), None),
            P(None, None, ("seqgrp", "fsdp")),
            P(("seqgrp", "fsdp"), "seq", None),
        ),
        out_specs=(
            P(("seqgrp", "fsdp"), "seq", None),
            P(("seqgrp", "fsdp"), "seq", None),
            P(("seqgrp", "fsdp")),
            P(("seqgrp", "fsdp")),
            P(("seqgrp", "fsdp"), None),
            P(("seqgrp", "fsdp"), None),
            P(("seqgrp", "fsdp"), None),
            P(("seqgrp", "fsdp"), None),
            P(("seqgrp", "fsdp"), None),
            P(None, ("seqgrp", "fsdp"), None),
            P(None, None, ("seqgrp", "fsdp")),
        ),
        check_vma=False,
    )
```

```python
import functools

import jax
import jax.numpy as jnp
from jax import lax
from jax.experimental import pallas as pl
from jax.experimental.pallas import tpu as pltpu
from jax.sharding import PartitionSpec as P

HEADS = 16
KV_HEADS = 8
HD = 64
FF = 512
EXPERTS = 3
EPS = 1e-06
THETA = 10000.0
NEG = -1e30
Y = ("seqgrp", "fsdp")
CORE = 2
HOPS = (1, 5, 4)
CHIPS = (0, 1, 4, 5)
OWN = (0, 1, 5, 4)
BF = jnp.bfloat16
F32 = jnp.float32
VMEM = 56 * 1024 * 1024


def dot(left, right):
    return jnp.dot(left, right, preferred_element_type=F32)


def dot_cols(left, right):
    return lax.dot_general(left, right, (((1,), (1,)), ((), ())), preferred_element_type=F32)


def dot_rows(left, right):
    return lax.dot_general(left, right, (((0,), (0,)), ((), ())), preferred_element_type=F32)


def lanes(rows, width=128):
    return lax.broadcasted_iota(jnp.int32, (rows, width), 1)


def swap_halves(u):
    lane = lanes(u.shape[0])
    return jnp.where((lane & 63) < 32, pltpu.roll(u, 96, 1), pltpu.roll(u, 32, 1))


def call(kernel, out_shape, scratch=(), smem=0, cost=None):
    def run(*args):
        count = len(args)
        return pl.pallas_call(
            kernel,
            out_shape=out_shape,
            in_specs=[pl.BlockSpec(memory_space=pltpu.SMEM)] * smem
            + [pl.BlockSpec(memory_space=pltpu.VMEM)] * (count - smem),
            out_specs=jax.tree.map(lambda _: pl.BlockSpec(memory_space=pltpu.VMEM), out_shape),
            scratch_shapes=list(scratch),
            compiler_params=pltpu.CompilerParams(vmem_limit_bytes=VMEM),
            cost_estimate=cost,
        )(*args)

    return run


def shape(*dims, kind=BF):
    return jax.ShapeDtypeStruct(dims, kind)


def cost(us):
    return pl.CostEstimate(flops=0, bytes_accessed=int(us * 3_600_000), transcendentals=0)


def pairs(k):
    return [(i, i ^ k) for i in range(8)]


def hop(x, k):
    return lax.ppermute(x, Y, pairs(k))


def gather_far(x):
    return {k: hop(x, k) for k in (4, 5, 1)}


def gather_near(x, far, *ready):
    parts = {0: x, CORE: hop(x, CORE), **far}
    for k in HOPS:
        parts[k ^ CORE] = hop(after(far[k], *ready) if k == 1 else far[k], CORE)
    return [parts[k] for k in range(8)]


def gather_group(x, *ready):
    return gather_near(x, gather_far(x), *ready)


def scatter_start(*blocks):
    mine, other = blocks[:4], hop(blocks[4], CORE)
    sums = [mine[i].astype(F32) + other[i].astype(F32) for i in range(4)]
    return [sums[0]] + [sums[i].astype(BF) for i in (1, 2, 3)]


def scatter_end(sums):
    return [sums[0]] + [hop(sums[i], OWN[i]) for i in (3, 2, 1)]


def total(parts):
    return parts[0] + sum(p.astype(F32) for p in parts[1:])


def after(x, *earlier):
    return lax.optimization_barrier((x,) + earlier)[0]


def norm_rows(x):
    return lax.rsqrt(jnp.mean(x * x, 1, keepdims=True) + EPS)


def join(even, odd):
    first = lanes(even.shape[0]) < 64
    even, odd = even.astype(F32), odd.astype(F32)
    low = jnp.where(first, even, pltpu.roll(odd, 64, 1))
    high = jnp.where(first, pltpu.roll(even, 64, 1), odd)
    return low.astype(BF), high.astype(BF)


def prepare_kernel(at_ref, wq_ref, wk_ref, wv_ref, small_ref, in_ref, out_ref, mine_ref, other_ref):
    me = at_ref[2]

    def put(y, block):
        k = me ^ y
        at = ((k >> 2) & 1) * 2 + (k & 1)

        @pl.when(((k >> 1) & 1) == 0)
        def own_core():
            mine_ref[at] = block

        @pl.when(((k >> 1) & 1) == 1)
        def other_core():
            other_ref[at] = block

    for t in range(4):
        at = slice(128 * t, 128 * t + 128)
        up = slice(512 + 128 * t, 640 + 128 * t)
        kvs = join(wk_ref[:, at], wv_ref[:, at])
        ins = join(in_ref[0, :, at], in_ref[0, :, up])
        for i in range(2):
            y = 2 * t + i
            query = wq_ref[:, 128 * y : 128 * y + 128]
            put(y, jnp.concatenate([query, kvs[i], small_ref[...], ins[i], out_ref[0, y]], 0))


def prepare(seq, me, wq, wk, wv, small, w_in, w_out):
    piece = jnp.minimum(seq, 11)
    at = jnp.stack([piece // 4, piece % 4, me]).astype(jnp.int32)

    def whole(*dims):
        return pl.BlockSpec(dims, lambda i, ref: (0,) * len(dims))

    return pl.pallas_call(
        prepare_kernel,
        grid_spec=pltpu.PrefetchScalarGridSpec(
            num_scalar_prefetch=1,
            grid=(1,),
            in_specs=[
                whole(128, 1024),
                whole(128, 512),
                whole(128, 512),
                whole(16, 128),
                pl.BlockSpec((1, 32, 1024), lambda i, ref: (ref[0], ref[1], 0)),
                pl.BlockSpec((1, 8, 16, 128), lambda i, ref: (ref[0], 0, ref[1], 0)),
            ],
            out_specs=[whole(4, 320, 128), whole(4, 320, 128)],
        ),
        out_shape=[shape(4, 320, 128), shape(4, 320, 128)],
        compiler_params=pltpu.CompilerParams(vmem_limit_bytes=VMEM),
        cost_estimate=cost(20),
    )(at, wq, wk, wv, small, w_in, w_out.reshape(3, 8, 64, 128))


def arrange_weights_kernel(all_ref, w1_ref, w2_ref):
    w2_ref[192:256, :] = jnp.zeros((64, 1024), BF)
    for y in range(8):
        ends = []
        for e in range(EXPERTS):
            ends.append(
                jnp.concatenate([all_ref[4 * e + i, y, :32, :] for i in range(4)], 0)
            )
        span = slice(128 * y, 128 * y + 128)
        low, high = join(ends[0], ends[1])
        w1_ref[span, :128] = low
        w1_ref[span, 256:384] = high
        low, high = join(ends[2], jnp.zeros_like(ends[2]))
        w1_ref[span, 128:256] = low
        w1_ref[span, 384:512] = high
        for s in range(12):
            w2_ref[16 * s : 16 * s + 16, span] = all_ref[s, y, 32:48, :]


def qkv_kernel(*refs):
    me_ref, xs, (mine_ref, near_ref), fars = refs[0], refs[1:9], refs[9:11], refs[11:14]
    cos_ref, sin_ref, pay_ref, w_ref, n_ref, small_ref, rest_ref = refs[14:]
    blocks = [(0, mine_ref.at[0]), (CORE, near_ref.at[0])]
    for k, far in zip(CHIPS[1:], fars):
        blocks += [(k, far.at[0]), (k ^ CORE, far.at[1])]
    for k, block in blocks:
        source = me_ref[0] ^ k
        rows = pl.ds(pl.multiple_of(source * 128, 128), 128)
        w_ref[rows, :128] = block[:128, :]
        w_ref[rows, 128:] = block[128:256, :]
        small_ref[:, rows] = block[256:272, :].astype(F32)
        rest_ref[source] = block[272:320, :]
    gain = small_ref[0:1, :]
    cosine, sine = cos_ref[...], sin_ref[...]
    first = lanes(128) < 64
    for pair in range(4):
        x = jnp.concatenate([xs[2 * pair][...], xs[2 * pair + 1][...]], 0).astype(F32)
        normed = (x * norm_rows(x) * gain).astype(BF)
        n_ref[256 * pair : 256 * pair + 256, :] = normed
        both = dot(normed, w_ref[...])
        for i in range(2):
            k = 2 * pair + i
            query = both[128 * i : 128 * i + 128, :128]
            kv = both[128 * i : 128 * i + 128, 128:]
            query = ((query * cosine + swap_halves(query) * sine) * HD**-0.5).astype(BF)
            kv = jnp.where(first, kv * cosine + swap_halves(kv) * sine, kv).astype(BF)
            for half in range(2):
                for slot in range(2):
                    at = slot * 64 + half * 32
                    pay_ref[2 * k + half, slot * 32 : slot * 32 + 32, :] = query[at : at + 32]
                pay_ref[2 * k + half, 64:192, :] = kv


def double(kv):
    kv = kv.astype(F32)
    rolled = pltpu.roll(kv, 64, 1)
    first = lanes(kv.shape[0]) < 64
    return jnp.where(first, kv, rolled), jnp.where(first, rolled, kv)


def stack_heads(rows):
    first = lanes(rows.shape[0]) < 64
    zero = jnp.zeros_like(rows)
    return jnp.concatenate([jnp.where(first, rows, zero), jnp.where(first, zero, rows)], 0)


def merge_heads(stacked):
    half = stacked.shape[0] // 2
    return jnp.where(lanes(half) < 64, stacked[:half], stacked[half:])


def causal(half):
    key = lax.broadcasted_iota(jnp.int32, (256, 256), 0)
    row = lax.broadcasted_iota(jnp.int32, (256, 256), 1) & 127
    return key <= (row >> 5) * 64 + half * 32 + (row & 31)


def scores_of(k2, stacked, n, mask):
    raw = dot_cols(k2[:n], stacked)
    last = jnp.where(mask, raw[n - 256 :], NEG)
    return last if n == 256 else jnp.concatenate([raw[: n - 256], last], 0)


def place(order_ref, p):
    slot = order_ref[p]
    return slot >> 1, slot & 1


def attend_kernel(order_ref, pay_ref, out_ref, sorted_ref, log_ref, q_ref, kv_ref, k2_ref, v2t_ref):
    for p in range(32):
        s, i = place(order_ref, p)
        q_ref[32 * p : 32 * p + 32, :] = pay_ref[s, pl.ds(pl.multiple_of(i * 32, 32), 32), :]
        kv_ref[64 * p : 64 * p + 64, :] = pay_ref[s, pl.ds(pl.multiple_of(64 + i * 64, 64), 64), :]
    for j in range(8):
        k2, v2 = double(kv_ref[256 * j : 256 * j + 256, :])
        k2_ref[256 * j : 256 * j + 256, :] = k2.astype(BF)
        v2t_ref[:, 256 * j : 256 * j + 256] = v2.T.astype(BF)
    mask = causal(order_ref[32])
    for c in range(8):
        n = 256 * (c + 1)
        stacked = stack_heads(q_ref[128 * c : 128 * c + 128, :])
        scores = scores_of(k2_ref, stacked, n, mask)
        top = jnp.max(scores, 0, keepdims=True)
        weights = jnp.exp(scores - top)
        total = jnp.sum(weights, 0, keepdims=True)
        mixed = dot(v2t_ref[:, :n], weights.astype(BF)) / total
        log_ref[c : c + 1, :] = top + jnp.log(total)
        mixed = merge_heads(mixed.T)
        sorted_ref[128 * c : 128 * c + 128, :] = mixed
        for r in range(4):
            s, i = place(order_ref, 4 * c + r)
            out_ref[s, pl.ds(pl.multiple_of(i * 32, 32), 32), :] = mixed[32 * r : 32 * r + 32].astype(BF)


def attend_back_kernel(
    order_ref, dmix_ref, sorted_ref, log_ref, q_ref, kv_ref, out_ref, k2_ref, k2t_ref, v2_ref, dk_ref, dv_ref, d_ref
):
    for p in range(32):
        s, i = place(order_ref, p)
        d_ref[32 * p : 32 * p + 32, :] = dmix_ref[s, pl.ds(pl.multiple_of(i * 32, 32), 32), :]
    for j in range(8):
        k2, v2 = double(kv_ref[256 * j : 256 * j + 256, :])
        k2_ref[256 * j : 256 * j + 256, :] = k2.astype(BF)
        v2_ref[256 * j : 256 * j + 256, :] = v2.astype(BF)
        k2t_ref[:, 256 * j : 256 * j + 256] = k2.T.astype(BF)
    mask = causal(order_ref[32])
    for c in reversed(range(8)):
        n = 256 * (c + 1)
        stacked = stack_heads(q_ref[128 * c : 128 * c + 128, :])
        dmix = d_ref[128 * c : 128 * c + 128, :]
        dstacked = stack_heads(dmix)
        product = dmix.astype(F32) * sorted_ref[128 * c : 128 * c + 128, :]
        delta = jnp.sum(stack_heads(product).T, 0, keepdims=True)
        scores = scores_of(k2_ref, stacked, n, mask)
        probs = jnp.exp(scores - log_ref[c : c + 1, :])
        dprobs = dot_cols(v2_ref[:n], dstacked)
        dscores = (probs * (dprobs - delta)).astype(BF)
        dkeys = dot(dscores, stacked)
        dvalues = dot(probs.astype(BF), dstacked)
        if c == 7:
            dk_ref[...] = dkeys
            dv_ref[...] = dvalues
        else:
            dk_ref[:n] += dkeys
            dv_ref[:n] += dvalues
        dquery = merge_heads(dot(k2t_ref[:, :n], dscores).T) * HD**-0.5
        for r in range(4):
            s, i = place(order_ref, 4 * c + r)
            out_ref[s, pl.ds(pl.multiple_of(i * 32, 32), 32), :] = dquery[32 * r : 32 * r + 32].astype(BF)
    first = lanes(64) < 64
    for p in range(32):
        s, i = place(order_ref, p)
        dk = dk_ref[64 * p : 64 * p + 64, :]
        dv = dv_ref[64 * p : 64 * p + 64, :]
        both = jnp.where(first, dk + pltpu.roll(dk, 64, 1), dv + pltpu.roll(dv, 64, 1))
        out_ref[s, pl.ds(pl.multiple_of(64 + i * 64, 64), 64), :] = both.astype(BF)


def rows_of(ref, k):
    return jnp.concatenate(
        [ref[2 * k + half, slot * 32 : slot * 32 + 32, :] for slot in range(2) for half in range(2)], 0
    )


def expand(table):
    lane = lanes(table.shape[0], 256)
    return jnp.where(
        lane < 64,
        table[:, 0:1],
        jnp.where(lane < 128, table[:, 1:2], jnp.where(lane < 192, table[:, 2:3], 0.0)),
    )


CHUNK = 4


def split_blocks(block, k, mine_refs, other_ref):
    if k & CORE:
        other_ref[OWN.index(k ^ CORE)] = block
    else:
        mine_refs[OWN.index(k)][...] = block


def split_shapes(*dims):
    return (shape(*dims),) * 4 + (shape(4, *dims),)


def expert_kernel(*refs):
    xs, mixes, wos, cots = refs[:8], refs[8:16], refs[16:24], refs[24:32]
    w1_ref, w2_ref, small_ref, router_ref = refs[32:36]
    hid_ref, pay_ref = refs[36:38]
    mine_refs, other_ref, mmine_refs, mother_ref = refs[38:42], refs[42], refs[43:47], refs[47]
    db_ref, wo_ref, n_ref, dj_ref, cot_ref, hg_ref = refs[48:]
    for m in range(8):
        wo_ref[128 * m : 128 * m + 128, :] = wos[m][...]
        cot_ref[128 * m : 128 * m + 128, :] = cots[m][:, :1024]
    rows = 128 * CHUNK
    gain = small_ref[1:2, :]
    gain_grad = jnp.zeros((1, 1024), F32)
    lane = lanes(rows)
    lane2 = lanes(rows, 256)
    for first in range(0, 8, CHUNK):
        ks = range(first, first + CHUNK)
        span = slice(128 * first, 128 * first + rows)
        x = jnp.concatenate([xs[k][...] for k in ks], 0).astype(F32)
        mixed = jnp.concatenate(
            [
                jnp.concatenate([rows_of(mixes[m], k ^ m) for m in range(8)], 1)
                for k in ks
            ],
            0,
        )
        hidden1 = x + dot(mixed, wo_ref[...])
        if first == 0:
            hid_ref[...] = hidden1[:128]
        scale = norm_rows(hidden1)
        unit = hidden1 * scale
        normed = (unit * gain).astype(BF)
        n_ref[span, :] = normed
        joint = dot(normed, w1_ref[...])
        logits = dot_cols(normed, router_ref[...])
        member = jnp.concatenate([cots[k][:, 1024:] for k in ks], 0).astype(F32) > 0.5
        logits = jnp.where(member, logits, NEG)
        weights = jnp.where(member, jnp.exp(logits - jnp.max(logits, 1, keepdims=True)), 0.0)
        gates = weights / jnp.sum(weights, 1, keepdims=True)
        spread = expand(gates)
        gate, up = joint[:, :256], joint[:, 256:]
        sigma = jax.nn.sigmoid(gate)
        active = gate * sigma
        hidden = (active * up).astype(BF).astype(F32)
        gated = (hidden * spread).astype(BF)
        hg_ref[span, :] = gated
        mixture = dot(gated, w2_ref[...]).astype(BF)
        draw = dot_cols(cot_ref[span, :], w2_ref[...])
        product = hidden * draw
        dgates = jnp.zeros((rows, 128), F32)
        for e in range(EXPERTS):
            part = jnp.sum(jnp.where((lane2 >> 6) == e, product, 0.0), 1, keepdims=True)
            dgates = jnp.where(lane == e, part, dgates)
        dlogits = (gates * (dgates - jnp.sum(gates * dgates, 1, keepdims=True))).astype(BF)
        dhidden = draw * spread
        slope = sigma * (1.0 + gate * (1.0 - sigma))
        djoint = jnp.concatenate([dhidden * up * slope, dhidden * active], 1).astype(BF)
        dj_ref[span, :512] = djoint
        dj_ref[span, 512:] = dlogits
        dnormed = dot_cols(djoint, w1_ref[...]) + dot(dlogits, router_ref[...])
        gain_grad += jnp.sum(dnormed * unit, 0, keepdims=True)
        dunit = dnormed * gain
        dbranch = scale * (dunit - unit * jnp.mean(dunit * unit, 1, keepdims=True))
        if first == 0:
            dbranch = jnp.concatenate([dbranch[:128] + cot_ref[:128, :].astype(F32), dbranch[128:]], 0)
        dbranch = dbranch.astype(BF)
        db_ref[span, :] = dbranch
        dmixed = dot_cols(dbranch, wo_ref[...]).astype(BF)
        for i, k in enumerate(ks):
            split_blocks(mixture[128 * i : 128 * i + 128], k, mmine_refs, mother_ref)
            for m in range(8):
                block = dmixed[128 * i : 128 * i + 128, 128 * m : 128 * m + 128]
                target = other_ref.at[OWN.index(m ^ CORE)] if m & CORE else mine_refs[OWN.index(m)]
                for half in range(2):
                    for slot in range(2):
                        at = slot * 64 + half * 32
                        target[2 * (k ^ m) + half, slot * 32 : slot * 32 + 32, :] = block[at : at + 32]
    grad1 = dot_rows(dj_ref[...], n_ref[...])
    pay_ref[:192, :] = grad1[:192].astype(BF)
    pay_ref[192:384, :] = grad1[256:448].astype(BF)
    last = grad1[512:576]
    row = lax.broadcasted_iota(jnp.int32, last.shape, 0)
    pay_ref[576:640, :] = jnp.where(row == 3, gain_grad, last).astype(BF)
    pay_ref[384:576, :] = dot_rows(hg_ref[...], cot_ref[...])[:192].astype(BF)


def wo_grad_kernel(*refs):
    mixes, db_ref, mine_refs, other_ref = refs[:8], refs[8], refs[9:13], refs[13]
    for m in range(8):
        mixed = jnp.concatenate([rows_of(mixes[m], k ^ m) for k in range(8)], 0)
        split_blocks(dot_rows(mixed, db_ref[...]).astype(BF), m, mine_refs, other_ref)


def by_chip(me, y, block, mine_ref, other_ref):
    k = me ^ y
    at = ((k >> 2) & 1) * 2 + (k & 1)

    @pl.when(((k >> 1) & 1) == 0)
    def own_core():
        mine_ref[at] = block

    @pl.when(((k >> 1) & 1) == 1)
    def other_core():
        other_ref[at] = block


def sum_kernel(me_ref, in_ref, mine_ref, other_ref):
    grad = jnp.zeros((40, 1024), F32)
    for s in range(16):
        grad += in_ref[s].astype(F32)
    grad = jnp.concatenate([grad, jnp.zeros((8, 1024), F32)], 0).astype(BF)
    for y in range(8):
        by_chip(me_ref[0], y, grad[:, 128 * y : 128 * y + 128], mine_ref, other_ref)


def qkv_back_kernel(*refs):
    xs, wos, (pay_ref, n_ref, cos_ref, sin_ref, w_ref, db_ref, small_ref) = refs[:8], refs[8:12], refs[12:19]
    g_ref, gn_ref, mine_refs, other_ref, d_ref = refs[19], refs[20], refs[21:25], refs[25], refs[26]
    gain = small_ref[0:1, :]
    grad_wo = wos[0][...] + sum(part[...].astype(F32) for part in wos[1:])
    grad_wo = grad_wo.T.astype(BF)
    cosine, sine = cos_ref[...], sin_ref[...]
    first = lanes(128) < 64
    for k in range(8):
        at = 128 * k
        dquery = rows_of(pay_ref, k).astype(F32)
        dquery = dquery * cosine - swap_halves(dquery) * sine
        dkv = pay_ref[2 * k, 64:192, :].astype(F32) + pay_ref[2 * k + 1, 64:192, :].astype(F32)
        dkv = jnp.where(first, dkv * cosine - swap_halves(dkv) * sine, dkv)
        d_ref[at : at + 128, :128] = dquery.astype(BF)
        d_ref[at : at + 128, 128:] = dkv.astype(BF)
    grad = dot_rows(d_ref[...], n_ref[...]).astype(BF)
    for s in range(16):
        for y in range(8):
            g_ref[s, 16 * y : 16 * y + 16, :] = grad[16 * s : 16 * s + 16, 128 * y : 128 * y + 128]
        g_ref[s, 128:, :] = grad_wo[64 * s : 64 * s + 64, :]
    gain_grad = jnp.zeros((1, 1024), F32)
    for pair in range(4):
        x = jnp.concatenate([xs[2 * pair][...], xs[2 * pair + 1][...]], 0).astype(F32)
        dnormed = dot_cols(d_ref[256 * pair : 256 * pair + 256, :], w_ref[...])
        scale = norm_rows(x)
        unit = x * scale
        gain_grad += jnp.sum(dnormed * unit, 0, keepdims=True)
        dunit = dnormed * gain
        dnormed = scale * (dunit - unit * jnp.mean(dunit * unit, 1, keepdims=True))
        dnormed = (dnormed + db_ref[256 * pair : 256 * pair + 256, :].astype(F32)).astype(BF)
        for i in range(2):
            split_blocks(dnormed[128 * i : 128 * i + 128], 2 * pair + i, mine_refs, other_ref)
    for y in range(8):
        part = gain_grad[:, 128 * y : 128 * y + 128]
        gn_ref[y] = jnp.broadcast_to(part, (16, 128)).astype(BF)


def qkv_final_kernel(all_ref, q_ref, k_ref, v_ref, wo_ref, gn_ref):
    first = lanes(128) < 64
    total = jnp.zeros((16, 128), F32)
    for s in range(16):
        total += all_ref[s, 128:144, :].astype(F32)
    gn_ref[...] = total[0:1]
    for s in range(0, 16, 2):
        rows = jnp.concatenate([all_ref[s, 144:208, :], all_ref[s + 1, 144:208, :]], 0)
        wo_ref[:, 64 * s : 64 * s + 128] = rows.astype(F32).T
    for t in range(4):
        tails = []
        for y in (2 * t, 2 * t + 1):
            rows = jnp.concatenate([all_ref[s, 16 * y : 16 * y + 16, :] for s in range(16)], 0)
            turned = rows.astype(F32).T
            q_ref[:, 128 * y : 128 * y + 128] = turned[:, :128]
            tails.append(turned[:, 128:])
        even, odd = tails
        k_ref[:, 128 * t : 128 * t + 128] = jnp.where(first, even, pltpu.roll(odd, 64, 1))
        v_ref[:, 128 * t : 128 * t + 128] = jnp.where(first, pltpu.roll(even, 64, 1), odd)


def expert_final_kernel(me_ref, in_ref, win_ref, wout_ref, router_ref, gn_ref, all_ref):
    for s in range(16):
        for k in range(8):
            part = in_ref[k, 48 * s : 48 * s + 40, :].astype(F32)
            all_ref[me_ref[0] ^ k, 40 * s : 40 * s + 40, :] = part
    for e in range(EXPERTS):
        for part in range(2):
            at = part * 192 + e * 64
            for t in range(4):
                rows = jnp.concatenate(
                    [all_ref[2 * t, at : at + 64, :], all_ref[2 * t + 1, at : at + 64, :]], 0
                )
                win_ref[e, :, part * 512 + 128 * t : part * 512 + 128 * t + 128] = rows.T
        for y in range(8):
            at = 384 + e * 64
            wout_ref[e, 64 * y : 64 * y + 64, :] = all_ref[y, at : at + 64, :]
    total = jnp.zeros((8, 128), F32)
    for y in range(8):
        total += all_ref[y, 576:584, :]
    router_ref[...] = total[:3]
    gn_ref[...] = total[3:4]


def swap_seq(x):
    return lax.all_to_all(x, "seq", 0, 0)


def swap_group(x):
    return lax.all_to_all(x, Y, 0, 0)


def spread_seq(x):
    return swap_seq(jnp.broadcast_to(x[None], (16,) + x.shape))


def local(
    tokens, block_order, routes, norm1, norm2, wq, wk, wv, wo, router, w_in, w_out, cotangent
):
    here = tokens[0]
    seq = lax.axis_index("seq")

    slots = lax.dynamic_slice_in_dim(block_order, 2 * seq, 2)
    position = (slots[:, None] * 64 + jnp.arange(64, dtype=jnp.int32)[None, :]).reshape(-1)
    freqs = THETA ** (-(jnp.arange(HD // 2, dtype=F32) * 2.0) / HD)
    angle = position.astype(F32)[:, None] * jnp.tile(freqs, 4)[None, :]
    cosine = jnp.cos(angle)
    sine = jnp.where((jnp.arange(128) & 63)[None, :] < 32, -jnp.sin(angle), jnp.sin(angle))
    index = jnp.arange(32, dtype=jnp.int32)
    order = jnp.sum(jnp.where(block_order[None, :] == index[:, None], index[None, :], 0), 1)
    order = jnp.concatenate([order, (seq & 1)[None].astype(jnp.int32)])
    member = jnp.any(
        routes[0][:, :, None] == jnp.arange(128, dtype=jnp.int32)[None, None, :], 1
    ).astype(BF)
    cot_member = jnp.concatenate([cotangent[0], member], 1)

    xs = gather_group(here)
    small = jnp.concatenate([norm1[None], norm2[None], router.T, jnp.zeros((11, 128), BF)], 0)
    me = lax.axis_index(Y).astype(jnp.int32)
    mine, near = prepare(seq, me, wq, wk, wv, small, w_in, w_out)
    near = hop(near, CORE)
    fars = [jnp.stack([mine[i], near[i]]) for i in (1, 2, 3)]
    fars = lax.optimization_barrier(
        (*fars, xs[1], xs[5], xs[4], cosine, sine, order, cot_member)
    )[:3]
    fars = [hop(far, k) for far, k in zip(fars, CHIPS[1:])]

    payload, w_qkv, normed1, gains, piece = call(
        qkv_kernel,
        (
            shape(16, 192, 128),
            shape(1024, 256),
            shape(1024, 1024),
            shape(16, 1024, kind=F32),
            shape(8, 48, 128),
        ),
        smem=1,
        cost=cost(1),
    )(me[None], *xs, mine, near, *fars, cosine, sine)

    expert_all = lax.all_gather(piece, "seq")
    w1, w2 = call(
        arrange_weights_kernel, (shape(1024, 512), shape(256, 1024)), cost=cost(1)
    )(expert_all)
    router_t = jnp.pad(gains[2:5].astype(BF), ((0, 125), (0, 0)))

    payload = swap_seq(payload)
    mixed_back, mixed_sorted, logs, q_sorted, kv_sorted = call(
        attend_kernel,
        (
            shape(16, 64, 128),
            shape(1024, 128, kind=F32),
            shape(8, 256, kind=F32),
            shape(1024, 128),
            shape(2048, 128),
        ),
        scratch=[pltpu.VMEM((2048, 128), BF), pltpu.VMEM((128, 2048), BF)],
        smem=1,
        cost=cost(1),
    )(order, payload)
    cots = gather_group(after(cot_member, xs[4]))
    wos = gather_group(after(wo, cots[4]))
    mixed_own = swap_seq(mixed_back)
    mixes = gather_group(mixed_own, w1, w2, router_t)
    hidden1, grad_pay, *partial = call(
        expert_kernel,
        (shape(128, 1024, kind=F32), shape(640, 1024))
        + split_shapes(16, 64, 128)
        + split_shapes(128, 1024)
        + (shape(1024, 1024),),
        scratch=[
            pltpu.VMEM((1024, 1024), BF),
            pltpu.VMEM((1024, 1024), BF),
            pltpu.VMEM((1024, 640), BF),
            pltpu.VMEM((1024, 1024), BF),
            pltpu.VMEM((1024, 256), BF),
        ],
        cost=cost(1),
    )(*xs, *mixes, *wos, *cots, w1, w2, gains, router_t)

    grad_pay = swap_seq(grad_pay.reshape(16, 40, 1024))
    dmix_parts = scatter_end(scatter_start(*partial[:5]))
    mixture, dbranch = partial[5:10], partial[10]
    dmix_pay = total(dmix_parts).astype(BF)

    wo_partial = call(wo_grad_kernel, split_shapes(128, 1024), cost=cost(1))(
        *mixes, after(dbranch, dmix_pay)
    )
    mine, near = call(
        sum_kernel, (shape(4, 48, 128), shape(4, 48, 128)), smem=1, cost=cost(1)
    )(me[None], after(grad_pay, dmix_pay))
    dmix_pay = after(swap_seq(dmix_pay), wo_partial[4], mine)
    back_pay = call(
        attend_back_kernel,
        shape(16, 192, 128),
        scratch=[
            pltpu.VMEM((2048, 128), BF),
            pltpu.VMEM((128, 2048), BF),
            pltpu.VMEM((2048, 128), BF),
            pltpu.VMEM((2048, 128), F32),
            pltpu.VMEM((2048, 128), F32),
            pltpu.VMEM((1024, 128), BF),
        ],
        smem=1,
        cost=cost(1),
    )(order, dmix_pay, mixed_sorted, logs, q_sorted, kv_sorted)

    wo_sums = scatter_start(*wo_partial[:4], after(wo_partial[4], dmix_pay))
    near = hop(after(near, dmix_pay), CORE)
    mine = after(mine, back_pay, *wo_sums)
    fars = [hop(jnp.stack([mine[i], near[i]]), CHIPS[i]) for i in (1, 2, 3)]
    blocks = {0: mine[0], CORE: near[0]}
    for k, far in zip(CHIPS[1:], fars):
        blocks[k], blocks[k ^ CORE] = far[0], far[1]
    grad_part = jnp.stack([blocks[k] for k in range(8)])
    expert_grads = lax.all_gather(grad_part, "seq", axis=1, tiled=True)
    part_win, part_wout, part_router, part_gain2 = call(
        expert_final_kernel,
        (
            shape(3, 128, 1024, kind=F32),
            shape(3, 512, 128, kind=F32),
            shape(3, 128, kind=F32),
            shape(1, 128, kind=F32),
        ),
        scratch=[pltpu.VMEM((8, 640, 128), F32)],
        smem=1,
        cost=cost(1),
    )(me[None], expert_grads)

    wo_parts = scatter_end(wo_sums)
    back_pay = swap_seq(back_pay)
    grad_qkv, grad_gain1, *partial = call(
        qkv_back_kernel,
        (shape(16, 192, 128), shape(8, 16, 128)) + split_shapes(128, 1024),
        scratch=[pltpu.VMEM((1024, 256), BF)],
        cost=cost(2),
    )(*xs, *wo_parts, back_pay, normed1, cosine, sine, w_qkv, dbranch, gains)
    dn_parts = scatter_end(scatter_start(*partial))
    grad_qkv = after(swap_seq(grad_qkv), *dn_parts)
    qkv_sum = jnp.sum(grad_qkv.astype(F32), 0).astype(BF)
    wo_sum = qkv_sum[128:]
    qkv_part = swap_group(jnp.concatenate([qkv_sum[:128].reshape(8, 16, 128), grad_gain1], 1))
    grad_inputs = total(dn_parts)
    mix_parts = scatter_end(scatter_start(*mixture[:4], after(mixture[4], grad_qkv)))
    outcome = (hidden1 + total(mix_parts)).astype(BF)
    qkv_part = after(qkv_part, grad_inputs, part_win)
    gain1_part = jnp.sum(qkv_part[:, 16:].astype(F32), 0).astype(BF)
    qkv_all = spread_seq(
        jnp.concatenate(
            [qkv_part[:, :16].reshape(128, 128), gain1_part, wo_sum], 0
        )
    )
    part_q, part_k, part_v, part_wo, part_gain1 = call(
        qkv_final_kernel,
        (
            shape(128, 1024, kind=F32),
            shape(128, 512, kind=F32),
            shape(128, 512, kind=F32),
            shape(128, 1024, kind=F32),
            shape(1, 128, kind=F32),
        ),
        cost=cost(1),
    )(after(qkv_all, outcome))

    return (
        outcome[None],
        grad_inputs[None],
        part_gain1[0],
        part_gain2[0],
        part_q,
        part_k,
        part_v,
        part_wo,
        part_router.T,
        part_win,
        part_wout,
    )


def solution(mesh):
    return jax.shard_map(
        local,
        mesh=mesh,
        in_specs=(
            P(("seqgrp", "fsdp"), "seq", None),
            P(),
            P(("seqgrp", "fsdp"), "seq", None),
            P(("seqgrp", "fsdp")),
            P(("seqgrp", "fsdp")),
            P(("seqgrp", "fsdp"), None),
            P(("seqgrp", "fsdp"), None),
            P(("seqgrp", "fsdp"), None),
            P(("seqgrp", "fsdp"), None),
            P(("seqgrp", "fsdp"), None),
            P(None, ("seqgrp", "fsdp"), None),
            P(None, None, ("seqgrp", "fsdp")),
            P(("seqgrp", "fsdp"), "seq", None),
        ),
        out_specs=(
            P(("seqgrp", "fsdp"), "seq", None),
            P(("seqgrp", "fsdp"), "seq", None),
            P(("seqgrp", "fsdp")),
            P(("seqgrp", "fsdp")),
            P(("seqgrp", "fsdp"), None),
            P(("seqgrp", "fsdp"), None),
            P(("seqgrp", "fsdp"), None),
            P(("seqgrp", "fsdp"), None),
            P(("seqgrp", "fsdp"), None),
            P(None, ("seqgrp", "fsdp"), None),
            P(None, None, ("seqgrp", "fsdp")),
        ),
        check_vma=False,
    )
```

```python
import functools

import jax
import jax.numpy as jnp
from jax import lax
from jax.experimental import pallas as pl
from jax.experimental.pallas import tpu as pltpu
from jax.sharding import PartitionSpec as P

HEADS = 16
KV_HEADS = 8
HD = 64
FF = 512
EXPERTS = 3
EPS = 1e-06
THETA = 10000.0
NEG = -1e30
Y = ("seqgrp", "fsdp")
CORE = 2
HOPS = (1, 5, 4)
CHIPS = (0, 1, 4, 5)
OWN = (0, 1, 5, 4)
BF = jnp.bfloat16
F32 = jnp.float32
VMEM = 56 * 1024 * 1024


def dot(left, right):
    return jnp.dot(left, right, preferred_element_type=F32)


def dot_cols(left, right):
    return lax.dot_general(left, right, (((1,), (1,)), ((), ())), preferred_element_type=F32)


def dot_rows(left, right):
    return lax.dot_general(left, right, (((0,), (0,)), ((), ())), preferred_element_type=F32)


def lanes(rows, width=128):
    return lax.broadcasted_iota(jnp.int32, (rows, width), 1)


def swap_halves(u):
    lane = lanes(u.shape[0])
    return jnp.where((lane & 63) < 32, pltpu.roll(u, 96, 1), pltpu.roll(u, 32, 1))


def call(kernel, out_shape, scratch=(), smem=0, cost=None):
    def run(*args):
        count = len(args)
        return pl.pallas_call(
            kernel,
            out_shape=out_shape,
            in_specs=[pl.BlockSpec(memory_space=pltpu.SMEM)] * smem
            + [pl.BlockSpec(memory_space=pltpu.VMEM)] * (count - smem),
            out_specs=jax.tree.map(lambda _: pl.BlockSpec(memory_space=pltpu.VMEM), out_shape),
            scratch_shapes=list(scratch),
            compiler_params=pltpu.CompilerParams(vmem_limit_bytes=VMEM),
            cost_estimate=cost,
        )(*args)

    return run


def shape(*dims, kind=BF):
    return jax.ShapeDtypeStruct(dims, kind)


def cost(us):
    return pl.CostEstimate(flops=0, bytes_accessed=int(us * 3_600_000), transcendentals=0)


def pairs(k):
    return [(i, i ^ k) for i in range(8)]


def hop(x, k):
    return lax.ppermute(x, Y, pairs(k))


def gather_far(x):
    return {k: hop(x, k) for k in (4, 5, 1)}


def gather_near(x, far, *ready):
    parts = {0: x, CORE: hop(x, CORE), **far}
    for k in HOPS:
        parts[k ^ CORE] = hop(after(far[k], *ready) if k == 1 else far[k], CORE)
    return [parts[k] for k in range(8)]


def gather_group(x, *ready):
    return gather_near(x, gather_far(x), *ready)


def scatter_start(*blocks):
    mine, other = blocks[:4], hop(blocks[4], CORE)
    sums = [mine[i].astype(F32) + other[i].astype(F32) for i in range(4)]
    return [sums[0]] + [sums[i].astype(BF) for i in (1, 2, 3)]


def scatter_end(sums):
    return [sums[0]] + [hop(sums[i], OWN[i]) for i in (3, 2, 1)]


def total(parts):
    return parts[0] + sum(p.astype(F32) for p in parts[1:])


def after(x, *earlier):
    return lax.optimization_barrier((x,) + earlier)[0]


def norm_rows(x):
    return lax.rsqrt(jnp.mean(x * x, 1, keepdims=True) + EPS)


def join(even, odd):
    first = lanes(even.shape[0]) < 64
    even, odd = even.astype(F32), odd.astype(F32)
    low = jnp.where(first, even, pltpu.roll(odd, 64, 1))
    high = jnp.where(first, pltpu.roll(even, 64, 1), odd)
    return low.astype(BF), high.astype(BF)


def prepare_kernel(at_ref, wq_ref, wk_ref, wv_ref, small_ref, in_ref, out_ref, mine_ref, other_ref):
    me = at_ref[2]

    def put(y, block):
        k = me ^ y
        at = ((k >> 2) & 1) * 2 + (k & 1)

        @pl.when(((k >> 1) & 1) == 0)
        def own_core():
            mine_ref[at] = block

        @pl.when(((k >> 1) & 1) == 1)
        def other_core():
            other_ref[at] = block

    for t in range(4):
        at = slice(128 * t, 128 * t + 128)
        up = slice(512 + 128 * t, 640 + 128 * t)
        kvs = join(wk_ref[:, at], wv_ref[:, at])
        ins = join(in_ref[0, :, at], in_ref[0, :, up])
        for i in range(2):
            y = 2 * t + i
            query = wq_ref[:, 128 * y : 128 * y + 128]
            put(y, jnp.concatenate([query, kvs[i], small_ref[...], ins[i], out_ref[0, y]], 0))


def prepare(seq, me, wq, wk, wv, small, w_in, w_out):
    piece = jnp.minimum(seq, 11)
    at = jnp.stack([piece // 4, piece % 4, me]).astype(jnp.int32)

    def whole(*dims):
        return pl.BlockSpec(dims, lambda i, ref: (0,) * len(dims))

    return pl.pallas_call(
        prepare_kernel,
        grid_spec=pltpu.PrefetchScalarGridSpec(
            num_scalar_prefetch=1,
            grid=(1,),
            in_specs=[
                whole(128, 1024),
                whole(128, 512),
                whole(128, 512),
                whole(16, 128),
                pl.BlockSpec((1, 32, 1024), lambda i, ref: (ref[0], ref[1], 0)),
                pl.BlockSpec((1, 8, 16, 128), lambda i, ref: (ref[0], 0, ref[1], 0)),
            ],
            out_specs=[whole(4, 320, 128), whole(4, 320, 128)],
        ),
        out_shape=[shape(4, 320, 128), shape(4, 320, 128)],
        compiler_params=pltpu.CompilerParams(vmem_limit_bytes=VMEM),
        cost_estimate=cost(20),
    )(at, wq, wk, wv, small, w_in, w_out.reshape(3, 8, 64, 128))


def arrange_weights_kernel(all_ref, w1_ref, w2_ref):
    w2_ref[192:256, :] = jnp.zeros((64, 1024), BF)
    for y in range(8):
        ends = []
        for e in range(EXPERTS):
            ends.append(
                jnp.concatenate([all_ref[4 * e + i, y, :32, :] for i in range(4)], 0)
            )
        span = slice(128 * y, 128 * y + 128)
        low, high = join(ends[0], ends[1])
        w1_ref[span, :128] = low
        w1_ref[span, 256:384] = high
        low, high = join(ends[2], jnp.zeros_like(ends[2]))
        w1_ref[span, 128:256] = low
        w1_ref[span, 384:512] = high
        for s in range(12):
            w2_ref[16 * s : 16 * s + 16, span] = all_ref[s, y, 32:48, :]


def qkv_kernel(*refs):
    me_ref, xs, (mine_ref, near_ref), fars = refs[0], refs[1:9], refs[9:11], refs[11:14]
    cos_ref, sin_ref, pay_ref, w_ref, n_ref, small_ref, rest_ref = refs[14:]
    blocks = [(0, mine_ref.at[0]), (CORE, near_ref.at[0])]
    for k, far in zip(CHIPS[1:], fars):
        blocks += [(k, far.at[0]), (k ^ CORE, far.at[1])]
    for k, block in blocks:
        source = me_ref[0] ^ k
        rows = pl.ds(pl.multiple_of(source * 128, 128), 128)
        w_ref[rows, :128] = block[:128, :]
        w_ref[rows, 128:] = block[128:256, :]
        small_ref[:, rows] = block[256:272, :].astype(F32)
        rest_ref[source] = block[272:320, :]
    gain = small_ref[0:1, :]
    cosine, sine = cos_ref[...], sin_ref[...]
    first = lanes(128) < 64
    for pair in range(4):
        x = jnp.concatenate([xs[2 * pair][...], xs[2 * pair + 1][...]], 0).astype(F32)
        normed = (x * norm_rows(x) * gain).astype(BF)
        n_ref[256 * pair : 256 * pair + 256, :] = normed
        both = dot(normed, w_ref[...])
        for i in range(2):
            k = 2 * pair + i
            query = both[128 * i : 128 * i + 128, :128]
            kv = both[128 * i : 128 * i + 128, 128:]
            query = ((query * cosine + swap_halves(query) * sine) * HD**-0.5).astype(BF)
            kv = jnp.where(first, kv * cosine + swap_halves(kv) * sine, kv).astype(BF)
            for half in range(2):
                for slot in range(2):
                    at = slot * 64 + half * 32
                    pay_ref[2 * k + half, slot * 32 : slot * 32 + 32, :] = query[at : at + 32]
                pay_ref[2 * k + half, 64:192, :] = kv


def double(kv):
    kv = kv.astype(F32)
    rolled = pltpu.roll(kv, 64, 1)
    first = lanes(kv.shape[0]) < 64
    return jnp.where(first, kv, rolled), jnp.where(first, rolled, kv)


def stack_heads(rows):
    first = lanes(rows.shape[0]) < 64
    zero = jnp.zeros_like(rows)
    return jnp.concatenate([jnp.where(first, rows, zero), jnp.where(first, zero, rows)], 0)


def merge_heads(stacked):
    half = stacked.shape[0] // 2
    return jnp.where(lanes(half) < 64, stacked[:half], stacked[half:])


def causal(half):
    key = lax.broadcasted_iota(jnp.int32, (256, 256), 0)
    row = lax.broadcasted_iota(jnp.int32, (256, 256), 1) & 127
    return key <= (row >> 5) * 64 + half * 32 + (row & 31)


def scores_of(k2, stacked, n, mask):
    raw = dot_cols(k2[:n], stacked)
    last = jnp.where(mask, raw[n - 256 :], NEG)
    return last if n == 256 else jnp.concatenate([raw[: n - 256], last], 0)


def place(order_ref, p):
    slot = order_ref[p]
    return slot >> 1, slot & 1


def attend_kernel(order_ref, pay_ref, out_ref, sorted_ref, log_ref, q_ref, kv_ref, k2_ref, v2t_ref):
    for p in range(32):
        s, i = place(order_ref, p)
        q_ref[32 * p : 32 * p + 32, :] = pay_ref[s, pl.ds(pl.multiple_of(i * 32, 32), 32), :]
        kv_ref[64 * p : 64 * p + 64, :] = pay_ref[s, pl.ds(pl.multiple_of(64 + i * 64, 64), 64), :]
    for j in range(8):
        k2, v2 = double(kv_ref[256 * j : 256 * j + 256, :])
        k2_ref[256 * j : 256 * j + 256, :] = k2.astype(BF)
        v2t_ref[:, 256 * j : 256 * j + 256] = v2.T.astype(BF)
    mask = causal(order_ref[32])
    for c in range(8):
        n = 256 * (c + 1)
        stacked = stack_heads(q_ref[128 * c : 128 * c + 128, :])
        scores = scores_of(k2_ref, stacked, n, mask)
        top = jnp.max(scores, 0, keepdims=True)
        weights = jnp.exp(scores - top)
        total = jnp.sum(weights, 0, keepdims=True)
        mixed = dot(v2t_ref[:, :n], weights.astype(BF)) / total
        log_ref[c : c + 1, :] = top + jnp.log(total)
        mixed = merge_heads(mixed.T)
        sorted_ref[128 * c : 128 * c + 128, :] = mixed
        for r in range(4):
            s, i = place(order_ref, 4 * c + r)
            out_ref[s, pl.ds(pl.multiple_of(i * 32, 32), 32), :] = mixed[32 * r : 32 * r + 32].astype(BF)


def attend_back_kernel(
    order_ref, dmix_ref, sorted_ref, log_ref, q_ref, kv_ref, out_ref, k2_ref, k2t_ref, v2_ref, dk_ref, dv_ref, d_ref
):
    for p in range(32):
        s, i = place(order_ref, p)
        d_ref[32 * p : 32 * p + 32, :] = dmix_ref[s, pl.ds(pl.multiple_of(i * 32, 32), 32), :]
    for j in range(8):
        k2, v2 = double(kv_ref[256 * j : 256 * j + 256, :])
        k2_ref[256 * j : 256 * j + 256, :] = k2.astype(BF)
        v2_ref[256 * j : 256 * j + 256, :] = v2.astype(BF)
        k2t_ref[:, 256 * j : 256 * j + 256] = k2.T.astype(BF)
    mask = causal(order_ref[32])
    for c in reversed(range(8)):
        n = 256 * (c + 1)
        stacked = stack_heads(q_ref[128 * c : 128 * c + 128, :])
        dmix = d_ref[128 * c : 128 * c + 128, :]
        dstacked = stack_heads(dmix)
        product = dmix.astype(F32) * sorted_ref[128 * c : 128 * c + 128, :]
        delta = jnp.sum(stack_heads(product).T, 0, keepdims=True)
        scores = scores_of(k2_ref, stacked, n, mask)
        probs = jnp.exp(scores - log_ref[c : c + 1, :])
        dprobs = dot_cols(v2_ref[:n], dstacked)
        dscores = (probs * (dprobs - delta)).astype(BF)
        dkeys = dot(dscores, stacked)
        dvalues = dot(probs.astype(BF), dstacked)
        if c == 7:
            dk_ref[...] = dkeys
            dv_ref[...] = dvalues
        else:
            dk_ref[:n] += dkeys
            dv_ref[:n] += dvalues
        dquery = merge_heads(dot(k2t_ref[:, :n], dscores).T) * HD**-0.5
        for r in range(4):
            s, i = place(order_ref, 4 * c + r)
            out_ref[s, pl.ds(pl.multiple_of(i * 32, 32), 32), :] = dquery[32 * r : 32 * r + 32].astype(BF)
    first = lanes(64) < 64
    for p in range(32):
        s, i = place(order_ref, p)
        dk = dk_ref[64 * p : 64 * p + 64, :]
        dv = dv_ref[64 * p : 64 * p + 64, :]
        both = jnp.where(first, dk + pltpu.roll(dk, 64, 1), dv + pltpu.roll(dv, 64, 1))
        out_ref[s, pl.ds(pl.multiple_of(64 + i * 64, 64), 64), :] = both.astype(BF)


def rows_of(ref, k):
    return jnp.concatenate(
        [ref[2 * k + half, slot * 32 : slot * 32 + 32, :] for slot in range(2) for half in range(2)], 0
    )


def expand(table):
    lane = lanes(table.shape[0], 256)
    return jnp.where(
        lane < 64,
        table[:, 0:1],
        jnp.where(lane < 128, table[:, 1:2], jnp.where(lane < 192, table[:, 2:3], 0.0)),
    )


CHUNK = 4


def split_blocks(block, k, mine_refs, other_ref):
    if k & CORE:
        other_ref[OWN.index(k ^ CORE)] = block
    else:
        mine_refs[OWN.index(k)][...] = block


def split_shapes(*dims):
    return (shape(*dims),) * 4 + (shape(4, *dims),)


def expert_kernel(*refs):
    xs, mixes, wos, cots = refs[:8], refs[8:16], refs[16:24], refs[24:32]
    w1_ref, w2_ref, small_ref, router_ref = refs[32:36]
    hid_ref, pay_ref = refs[36:38]
    mine_refs, other_ref, mmine_refs, mother_ref = refs[38:42], refs[42], refs[43:47], refs[47]
    db_ref, wo_ref, n_ref, dj_ref, cot_ref, hg_ref = refs[48:]
    for m in range(8):
        wo_ref[128 * m : 128 * m + 128, :] = wos[m][...]
        cot_ref[128 * m : 128 * m + 128, :] = cots[m][:, :1024]
    rows = 128 * CHUNK
    gain = small_ref[1:2, :]
    gain_grad = jnp.zeros((1, 1024), F32)
    lane = lanes(rows)
    lane2 = lanes(rows, 256)
    for first in range(0, 8, CHUNK):
        ks = range(first, first + CHUNK)
        span = slice(128 * first, 128 * first + rows)
        x = jnp.concatenate([xs[k][...] for k in ks], 0).astype(F32)
        mixed = jnp.concatenate(
            [
                jnp.concatenate([rows_of(mixes[m], k ^ m) for m in range(8)], 1)
                for k in ks
            ],
            0,
        )
        hidden1 = x + dot(mixed, wo_ref[...])
        if first == 0:
            hid_ref[...] = hidden1[:128]
        scale = norm_rows(hidden1)
        unit = hidden1 * scale
        normed = (unit * gain).astype(BF)
        n_ref[span, :] = normed
        joint = dot(normed, w1_ref[...])
        logits = dot_cols(normed, router_ref[...])
        member = jnp.concatenate([cots[k][:, 1024:] for k in ks], 0).astype(F32) > 0.5
        logits = jnp.where(member, logits, NEG)
        weights = jnp.where(member, jnp.exp(logits - jnp.max(logits, 1, keepdims=True)), 0.0)
        gates = weights / jnp.sum(weights, 1, keepdims=True)
        spread = expand(gates)
        gate, up = joint[:, :256], joint[:, 256:]
        sigma = jax.nn.sigmoid(gate)
        active = gate * sigma
        hidden = (active * up).astype(BF).astype(F32)
        gated = (hidden * spread).astype(BF)
        hg_ref[span, :] = gated
        mixture = dot(gated, w2_ref[...]).astype(BF)
        draw = dot_cols(cot_ref[span, :], w2_ref[...])
        product = hidden * draw
        dgates = jnp.zeros((rows, 128), F32)
        for e in range(EXPERTS):
            part = jnp.sum(jnp.where((lane2 >> 6) == e, product, 0.0), 1, keepdims=True)
            dgates = jnp.where(lane == e, part, dgates)
        dlogits = (gates * (dgates - jnp.sum(gates * dgates, 1, keepdims=True))).astype(BF)
        dhidden = draw * spread
        slope = sigma * (1.0 + gate * (1.0 - sigma))
        djoint = jnp.concatenate([dhidden * up * slope, dhidden * active], 1).astype(BF)
        dj_ref[span, :512] = djoint
        dj_ref[span, 512:] = dlogits
        dnormed = dot_cols(djoint, w1_ref[...]) + dot(dlogits, router_ref[...])
        gain_grad += jnp.sum(dnormed * unit, 0, keepdims=True)
        dunit = dnormed * gain
        dbranch = scale * (dunit - unit * jnp.mean(dunit * unit, 1, keepdims=True))
        if first == 0:
            dbranch = jnp.concatenate([dbranch[:128] + cot_ref[:128, :].astype(F32), dbranch[128:]], 0)
        dbranch = dbranch.astype(BF)
        db_ref[span, :] = dbranch
        dmixed = dot_cols(dbranch, wo_ref[...]).astype(BF)
        for i, k in enumerate(ks):
            split_blocks(mixture[128 * i : 128 * i + 128], k, mmine_refs, mother_ref)
            for m in range(8):
                block = dmixed[128 * i : 128 * i + 128, 128 * m : 128 * m + 128]
                target = other_ref.at[OWN.index(m ^ CORE)] if m & CORE else mine_refs[OWN.index(m)]
                for half in range(2):
                    for slot in range(2):
                        at = slot * 64 + half * 32
                        target[2 * (k ^ m) + half, slot * 32 : slot * 32 + 32, :] = block[at : at + 32]
    grad1 = dot_rows(dj_ref[...], n_ref[...])
    pay_ref[:192, :] = grad1[:192].astype(BF)
    pay_ref[192:384, :] = grad1[256:448].astype(BF)
    last = grad1[512:576]
    row = lax.broadcasted_iota(jnp.int32, last.shape, 0)
    pay_ref[576:640, :] = jnp.where(row == 3, gain_grad, last).astype(BF)
    pay_ref[384:576, :] = dot_rows(hg_ref[...], cot_ref[...])[:192].astype(BF)


def wo_grad_kernel(*refs):
    mixes, db_ref, mine_refs, other_ref = refs[:8], refs[8], refs[9:13], refs[13]
    for m in range(8):
        mixed = jnp.concatenate([rows_of(mixes[m], k ^ m) for k in range(8)], 0)
        split_blocks(dot_rows(mixed, db_ref[...]).astype(BF), m, mine_refs, other_ref)


def by_chip(me, y, block, mine_ref, other_ref):
    k = me ^ y
    at = ((k >> 2) & 1) * 2 + (k & 1)

    @pl.when(((k >> 1) & 1) == 0)
    def own_core():
        mine_ref[at] = block

    @pl.when(((k >> 1) & 1) == 1)
    def other_core():
        other_ref[at] = block


def sum_kernel(me_ref, in_ref, mine_ref, other_ref):
    grad = jnp.zeros((40, 1024), F32)
    for s in range(16):
        grad += in_ref[s].astype(F32)
    grad = jnp.concatenate([grad, jnp.zeros((8, 1024), F32)], 0).astype(BF)
    for y in range(8):
        by_chip(me_ref[0], y, grad[:, 128 * y : 128 * y + 128], mine_ref, other_ref)


def qkv_back_kernel(*refs):
    xs, wos, (pay_ref, n_ref, cos_ref, sin_ref, w_ref, db_ref, small_ref) = refs[:8], refs[8:12], refs[12:19]
    g_ref, gn_ref, mine_refs, other_ref, d_ref = refs[19], refs[20], refs[21:25], refs[25], refs[26]
    gain = small_ref[0:1, :]
    grad_wo = wos[0][...] + sum(part[...].astype(F32) for part in wos[1:])
    grad_wo = grad_wo.T.astype(BF)
    cosine, sine = cos_ref[...], sin_ref[...]
    first = lanes(128) < 64
    for k in range(8):
        at = 128 * k
        dquery = rows_of(pay_ref, k).astype(F32)
        dquery = dquery * cosine - swap_halves(dquery) * sine
        dkv = pay_ref[2 * k, 64:192, :].astype(F32) + pay_ref[2 * k + 1, 64:192, :].astype(F32)
        dkv = jnp.where(first, dkv * cosine - swap_halves(dkv) * sine, dkv)
        d_ref[at : at + 128, :128] = dquery.astype(BF)
        d_ref[at : at + 128, 128:] = dkv.astype(BF)
    grad = dot_rows(d_ref[...], n_ref[...]).astype(BF)
    for s in range(16):
        for y in range(8):
            g_ref[s, 16 * y : 16 * y + 16, :] = grad[16 * s : 16 * s + 16, 128 * y : 128 * y + 128]
        g_ref[s, 128:, :] = grad_wo[64 * s : 64 * s + 64, :]
    gain_grad = jnp.zeros((1, 1024), F32)
    for pair in range(4):
        x = jnp.concatenate([xs[2 * pair][...], xs[2 * pair + 1][...]], 0).astype(F32)
        dnormed = dot_cols(d_ref[256 * pair : 256 * pair + 256, :], w_ref[...])
        scale = norm_rows(x)
        unit = x * scale
        gain_grad += jnp.sum(dnormed * unit, 0, keepdims=True)
        dunit = dnormed * gain
        dnormed = scale * (dunit - unit * jnp.mean(dunit * unit, 1, keepdims=True))
        dnormed = (dnormed + db_ref[256 * pair : 256 * pair + 256, :].astype(F32)).astype(BF)
        for i in range(2):
            split_blocks(dnormed[128 * i : 128 * i + 128], 2 * pair + i, mine_refs, other_ref)
    for y in range(8):
        part = gain_grad[:, 128 * y : 128 * y + 128]
        gn_ref[y] = jnp.broadcast_to(part, (16, 128)).astype(BF)


def qkv_final_kernel(all_ref, q_ref, k_ref, v_ref, wo_ref, gn_ref):
    first = lanes(128) < 64
    total = jnp.zeros((16, 128), F32)
    for s in range(16):
        total += all_ref[s, 128:144, :].astype(F32)
    gn_ref[...] = total[0:1]
    for s in range(0, 16, 2):
        rows = jnp.concatenate([all_ref[s, 144:208, :], all_ref[s + 1, 144:208, :]], 0)
        wo_ref[:, 64 * s : 64 * s + 128] = rows.astype(F32).T
    for t in range(4):
        tails = []
        for y in (2 * t, 2 * t + 1):
            rows = jnp.concatenate([all_ref[s, 16 * y : 16 * y + 16, :] for s in range(16)], 0)
            turned = rows.astype(F32).T
            q_ref[:, 128 * y : 128 * y + 128] = turned[:, :128]
            tails.append(turned[:, 128:])
        even, odd = tails
        k_ref[:, 128 * t : 128 * t + 128] = jnp.where(first, even, pltpu.roll(odd, 64, 1))
        v_ref[:, 128 * t : 128 * t + 128] = jnp.where(first, pltpu.roll(even, 64, 1), odd)


def expert_final_kernel(me_ref, in_ref, win_ref, wout_ref, router_ref, gn_ref, all_ref):
    for s in range(16):
        for k in range(8):
            part = in_ref[k, 48 * s : 48 * s + 40, :].astype(F32)
            all_ref[me_ref[0] ^ k, 40 * s : 40 * s + 40, :] = part
    for e in range(EXPERTS):
        for part in range(2):
            at = part * 192 + e * 64
            for t in range(4):
                rows = jnp.concatenate(
                    [all_ref[2 * t, at : at + 64, :], all_ref[2 * t + 1, at : at + 64, :]], 0
                )
                win_ref[e, :, part * 512 + 128 * t : part * 512 + 128 * t + 128] = rows.T
        for y in range(8):
            at = 384 + e * 64
            wout_ref[e, 64 * y : 64 * y + 64, :] = all_ref[y, at : at + 64, :]
    total = jnp.zeros((8, 128), F32)
    for y in range(8):
        total += all_ref[y, 576:584, :]
    router_ref[...] = total[:3]
    gn_ref[...] = total[3:4]


def swap_seq(x):
    return lax.all_to_all(x, "seq", 0, 0)


def swap_group(x):
    return lax.all_to_all(x, Y, 0, 0)


def spread_seq(x):
    return swap_seq(jnp.broadcast_to(x[None], (16,) + x.shape))


def local(
    tokens, block_order, routes, norm1, norm2, wq, wk, wv, wo, router, w_in, w_out, cotangent
):
    here = tokens[0]
    seq = lax.axis_index("seq")

    slots = lax.dynamic_slice_in_dim(block_order, 2 * seq, 2)
    position = (slots[:, None] * 64 + jnp.arange(64, dtype=jnp.int32)[None, :]).reshape(-1)
    freqs = THETA ** (-(jnp.arange(HD // 2, dtype=F32) * 2.0) / HD)
    angle = position.astype(F32)[:, None] * jnp.tile(freqs, 4)[None, :]
    cosine = jnp.cos(angle)
    sine = jnp.where((jnp.arange(128) & 63)[None, :] < 32, -jnp.sin(angle), jnp.sin(angle))
    index = jnp.arange(32, dtype=jnp.int32)
    order = jnp.sum(jnp.where(block_order[None, :] == index[:, None], index[None, :], 0), 1)
    order = jnp.concatenate([order, (seq & 1)[None].astype(jnp.int32)])
    member = jnp.any(
        routes[0][:, :, None] == jnp.arange(128, dtype=jnp.int32)[None, None, :], 1
    ).astype(BF)
    cot_member = jnp.concatenate([cotangent[0], member], 1)

    xs = gather_group(here)
    small = jnp.concatenate([norm1[None], norm2[None], router.T, jnp.zeros((11, 128), BF)], 0)
    me = lax.axis_index(Y).astype(jnp.int32)
    mine, near = prepare(seq, me, wq, wk, wv, small, w_in, w_out)
    near = hop(near, CORE)
    fars = [jnp.stack([mine[i], near[i]]) for i in (1, 2, 3)]
    fars = lax.optimization_barrier(
        (*fars, xs[1], xs[5], xs[4], cosine, sine, order, cot_member)
    )[:3]
    fars = [hop(far, k) for far, k in zip(fars, CHIPS[1:])]

    payload, w_qkv, normed1, gains, piece = call(
        qkv_kernel,
        (
            shape(16, 192, 128),
            shape(1024, 256),
            shape(1024, 1024),
            shape(16, 1024, kind=F32),
            shape(8, 48, 128),
        ),
        smem=1,
        cost=cost(1),
    )(me[None], *xs, mine, near, *fars, cosine, sine)

    expert_all = lax.all_gather(piece, "seq")
    w1, w2 = call(
        arrange_weights_kernel, (shape(1024, 512), shape(256, 1024)), cost=cost(1)
    )(expert_all)
    router_t = jnp.pad(gains[2:5].astype(BF), ((0, 125), (0, 0)))

    payload = swap_seq(payload)
    mixed_back, mixed_sorted, logs, q_sorted, kv_sorted = call(
        attend_kernel,
        (
            shape(16, 64, 128),
            shape(1024, 128, kind=F32),
            shape(8, 256, kind=F32),
            shape(1024, 128),
            shape(2048, 128),
        ),
        scratch=[pltpu.VMEM((2048, 128), BF), pltpu.VMEM((128, 2048), BF)],
        smem=1,
        cost=cost(1),
    )(order, payload)
    cots = gather_group(after(cot_member, xs[4]))
    wos = gather_group(after(wo, cots[4]))
    mixed_own = swap_seq(mixed_back)
    mixes = gather_group(mixed_own, w1, w2, router_t)
    hidden1, grad_pay, *partial = call(
        expert_kernel,
        (shape(128, 1024, kind=F32), shape(640, 1024))
        + split_shapes(16, 64, 128)
        + split_shapes(128, 1024)
        + (shape(1024, 1024),),
        scratch=[
            pltpu.VMEM((1024, 1024), BF),
            pltpu.VMEM((1024, 1024), BF),
            pltpu.VMEM((1024, 640), BF),
            pltpu.VMEM((1024, 1024), BF),
            pltpu.VMEM((1024, 256), BF),
        ],
        cost=cost(1),
    )(*xs, *mixes, *wos, *cots, w1, w2, gains, router_t)

    grad_pay = swap_seq(grad_pay.reshape(16, 40, 1024))
    dmix_parts = scatter_end(scatter_start(*partial[:5]))
    mixture, dbranch = partial[5:10], partial[10]
    dmix_pay = total(dmix_parts).astype(BF)

    wo_partial = call(wo_grad_kernel, split_shapes(128, 1024), cost=cost(1))(
        *mixes, after(dbranch, dmix_pay)
    )
    mine, near = call(
        sum_kernel, (shape(4, 48, 128), shape(4, 48, 128)), smem=1, cost=cost(1)
    )(me[None], after(grad_pay, dmix_pay))
    dmix_pay = after(swap_seq(dmix_pay), wo_partial[4], mine)
    back_pay = call(
        attend_back_kernel,
        shape(16, 192, 128),
        scratch=[
            pltpu.VMEM((2048, 128), BF),
            pltpu.VMEM((128, 2048), BF),
            pltpu.VMEM((2048, 128), BF),
            pltpu.VMEM((2048, 128), F32),
            pltpu.VMEM((2048, 128), F32),
            pltpu.VMEM((1024, 128), BF),
        ],
        smem=1,
        cost=cost(1),
    )(order, dmix_pay, mixed_sorted, logs, q_sorted, kv_sorted)

    wo_sums = scatter_start(*wo_partial[:4], after(wo_partial[4], dmix_pay))
    near = hop(after(near, dmix_pay), CORE)
    mine = after(mine, back_pay, *wo_sums)
    fars = [hop(jnp.stack([mine[i], near[i]]), CHIPS[i]) for i in (1, 2, 3)]
    blocks = {0: mine[0], CORE: near[0]}
    for k, far in zip(CHIPS[1:], fars):
        blocks[k], blocks[k ^ CORE] = far[0], far[1]
    grad_part = jnp.stack([blocks[k] for k in range(8)])
    expert_grads = lax.all_gather(grad_part, "seq", axis=1, tiled=True)
    part_win, part_wout, part_router, part_gain2 = call(
        expert_final_kernel,
        (
            shape(3, 128, 1024, kind=F32),
            shape(3, 512, 128, kind=F32),
            shape(3, 128, kind=F32),
            shape(1, 128, kind=F32),
        ),
        scratch=[pltpu.VMEM((8, 640, 128), F32)],
        smem=1,
        cost=cost(1),
    )(me[None], expert_grads)

    wo_parts = scatter_end(wo_sums)
    back_pay = swap_seq(back_pay)
    grad_qkv, grad_gain1, *partial = call(
        qkv_back_kernel,
        (shape(16, 192, 128), shape(8, 16, 128)) + split_shapes(128, 1024),
        scratch=[pltpu.VMEM((1024, 256), BF)],
        cost=cost(2),
    )(*xs, *wo_parts, back_pay, normed1, cosine, sine, w_qkv, dbranch, gains)
    dn_parts = scatter_end(scatter_start(*partial))
    grad_qkv = after(swap_seq(grad_qkv), *dn_parts)
    qkv_sum = jnp.sum(grad_qkv.astype(F32), 0).astype(BF)
    wo_sum = qkv_sum[128:]
    qkv_part = swap_group(jnp.concatenate([qkv_sum[:128].reshape(8, 16, 128), grad_gain1], 1))
    grad_inputs = total(dn_parts)
    mix_parts = scatter_end(scatter_start(*mixture[:4], after(mixture[4], grad_qkv)))
    outcome = (hidden1 + total(mix_parts)).astype(BF)
    qkv_part = after(qkv_part, grad_inputs, part_win)
    gain1_part = jnp.sum(qkv_part[:, 16:].astype(F32), 0).astype(BF)
    qkv_all = spread_seq(
        jnp.concatenate(
            [qkv_part[:, :16].reshape(128, 128), gain1_part, wo_sum], 0
        )
    )
    part_q, part_k, part_v, part_wo, part_gain1 = call(
        qkv_final_kernel,
        (
            shape(128, 1024, kind=F32),
            shape(128, 512, kind=F32),
            shape(128, 512, kind=F32),
            shape(128, 1024, kind=F32),
            shape(1, 128, kind=F32),
        ),
        cost=cost(1),
    )(qkv_all)

    return (
        outcome[None],
        grad_inputs[None],
        part_gain1[0],
        part_gain2[0],
        part_q,
        part_k,
        part_v,
        part_wo,
        part_router.T,
        part_win,
        part_wout,
    )


def solution(mesh):
    return jax.shard_map(
        local,
        mesh=mesh,
        in_specs=(
            P(("seqgrp", "fsdp"), "seq", None),
            P(),
            P(("seqgrp", "fsdp"), "seq", None),
            P(("seqgrp", "fsdp")),
            P(("seqgrp", "fsdp")),
            P(("seqgrp", "fsdp"), None),
            P(("seqgrp", "fsdp"), None),
            P(("seqgrp", "fsdp"), None),
            P(("seqgrp", "fsdp"), None),
            P(("seqgrp", "fsdp"), None),
            P(None, ("seqgrp", "fsdp"), None),
            P(None, None, ("seqgrp", "fsdp")),
            P(("seqgrp", "fsdp"), "seq", None),
        ),
        out_specs=(
            P(("seqgrp", "fsdp"), "seq", None),
            P(("seqgrp", "fsdp"), "seq", None),
            P(("seqgrp", "fsdp")),
            P(("seqgrp", "fsdp")),
            P(("seqgrp", "fsdp"), None),
            P(("seqgrp", "fsdp"), None),
            P(("seqgrp", "fsdp"), None),
            P(("seqgrp", "fsdp"), None),
            P(("seqgrp", "fsdp"), None),
            P(None, ("seqgrp", "fsdp"), None),
            P(None, None, ("seqgrp", "fsdp")),
        ),
        check_vma=False,
    )
```
